512 devices in a mesh: mode: 64 (over z_lo, y, core), row: 8 (over z_hi, x).
Axes of the slice: x: 4, y: 4, z: 16 (z_hi: 2, z_lo: 8; z = z_hi * 8 + z_lo), core: 2. Of those that a mesh axis runs over, the one named last changes fastest.
Arguments:
- forward: bfloat16 [64, 2, 1024, 1024], P('mode', None, 'row'), may hold values from -8 to 8
- backward_first: bfloat16 [64, 2, 1024, 1024], P('mode', None, 'row'), may hold values from -8 to 8
- backward_second: bfloat16 [64, 2, 1024, 1024], P('mode', None, 'row'), may hold values from -8 to 8
- phase_first: float32 [1024, 1024], P('row'), may hold values from -3.140625 to 3.140625
- phase_second: float32 [1024, 1024], P('row'), may hold values from -3.140625 to 3.140625
Outputs:
- mask_first: bfloat16 [2, 1024, 1024], P(None, 'row')
- mask_second: bfloat16 [2, 1024, 1024], P(None, 'row')
- arrived: bfloat16 [64, 2, 1024, 1024], P('mode', None, 'row')
The draws below stay inside these ranges and needn't reach their ends.
All inputs are finite; a program needn't handle non-finite values.
Results may differ from the reference program's by a relative error of at most 0.03.
Values may be sent and summed in bfloat16 or wider, within the bound.
A program may use at most 64 MiB of HBM per device.

```python
import math
import jax
import jax.numpy as jnp
from jax import lax

GRID = 1024
MODES = 64


def field_draw(key, spread):
    keys = jax.random.split(key, 5)
    base = jax.random.normal(keys[0], (MODES, 2, GRID, GRID), jnp.float32)
    ramp = jnp.exp(jnp.arange(GRID, dtype=jnp.float32) * (math.log(3.0) / GRID))
    row_scale = jnp.exp(jax.random.uniform(keys[2], (GRID,), jnp.float32, 0.0, math.log(spread))) * ramp
    col_scale = jnp.exp(jax.random.uniform(keys[3], (GRID,), jnp.float32, 0.0, math.log(spread)))
    mode_scale = jnp.exp(jax.random.uniform(keys[4], (MODES, 1, 1, 1), jnp.float32, -0.5, 0.5))
    values = base * row_scale[:, None] * col_scale[None, :] * mode_scale / (2.0 * spread)
    return jnp.clip(values, -8.0, 8.0).astype(jnp.bfloat16)


def draw_forward(key, part):
    key = jax.random.fold_in(key, 11)
    return field_draw(key, 10.0)


def draw_backward_first(key, part):
    key = jax.random.fold_in(key, 23)
    return field_draw(key, 10.0)


def draw_backward_second(key, part):
    key = jax.random.fold_in(key, 37)
    return field_draw(key, 10.0)


def setup_inputs(seed: int = 0) -> dict:
    arg_keys = jax.random.split(jax.random.key(seed), 6)
    return {
        "forward": draw_forward(jax.random.fold_in(arg_keys[5], 71), 0),
        "backward_first": draw_backward_first(jax.random.fold_in(arg_keys[5], 71), 0),
        "backward_second": draw_backward_second(jax.random.fold_in(arg_keys[5], 71), 0),
        "phase_first": jnp.clip(jax.random.uniform(arg_keys[3], (GRID, GRID), jnp.float32, -3.140625, 3.140625), -3.140625, 3.140625),
        "phase_second": jnp.clip(jax.random.uniform(arg_keys[4], (GRID, GRID), jnp.float32, -3.140625, 3.140625), -3.140625, 3.140625),
    }


def make_tables(grid_size):
    indices = jnp.arange(grid_size, dtype=jnp.int32)
    turns = indices[:, None] * indices[None, :] % grid_size
    angles = turns.astype(jnp.float32) * (2.0 * math.pi / grid_size)
    cosine = jnp.cos(angles).astype(jnp.bfloat16)
    sine_table = jnp.sin(angles).astype(jnp.bfloat16)
    frequency = (indices + grid_size // 2) % grid_size - grid_size // 2
    phases = (frequency * frequency % (2 * grid_size)).astype(jnp.float32) * (math.pi / grid_size)
    return (cosine, sine_table, jnp.cos(phases), -jnp.sin(phases))

def transform(field, tables, direct, along_rows):
    cosine, sine_table, chirp_real, chirp_imag = tables
    values = field.astype(jnp.float32)
    cos_full = cosine.astype(jnp.float32)
    sin_full = sine_table.astype(jnp.float32)
    if along_rows:
        with_cos = jnp.einsum('uk,mpkc->mpuc', cos_full, values, precision=lax.Precision.HIGHEST)
        with_sin = jnp.einsum('uk,mpkc->mpuc', sin_full, values, precision=lax.Precision.HIGHEST)
        factor_real = chirp_real[:, None]
        factor_imag = chirp_imag[:, None]
    else:
        with_cos = jnp.einsum('mpru,uk->mprk', values, cos_full, precision=lax.Precision.HIGHEST)
        with_sin = jnp.einsum('mpru,uk->mprk', values, sin_full, precision=lax.Precision.HIGHEST)
        factor_real = chirp_real
        factor_imag = chirp_imag
    if direct:
        part_real = with_cos[:, 0] + with_sin[:, 1]
        part_imag = with_cos[:, 1] - with_sin[:, 0]
        out_real = part_real * factor_real - part_imag * factor_imag
        out_imag = part_real * factor_imag + part_imag * factor_real
    else:
        length = cosine.shape[0]
        out_real = (with_cos[:, 0] - with_sin[:, 1]) / length
        out_imag = (with_cos[:, 1] + with_sin[:, 0]) / length
    return jnp.stack([out_real, out_imag], axis=1).astype(jnp.bfloat16)

def products(front_one, back_one):
    front_real = front_one[0].astype(jnp.float32)
    front_imag = front_one[1].astype(jnp.float32)
    back_real = back_one[0].astype(jnp.float32)
    back_imag = back_one[1].astype(jnp.float32)
    return (back_real * front_real + back_imag * front_imag, back_real * front_imag - back_imag * front_real)

def new_mask(front, back, phase):
    cos_phase = jnp.cos(phase)
    sin_phase = jnp.sin(phase)

    def intersection(pair):
        prod_real, prod_imag = products(pair[0], pair[1])
        return jnp.stack([jnp.sum(prod_real * cos_phase - prod_imag * sin_phase), jnp.sum(prod_real * sin_phase + prod_imag * cos_phase)])
    intersections = lax.map(intersection, (front, back))

    def accumulate(carry, item):
        prod_real, prod_imag = products(item[0], item[1])
        over = item[2]
        return ((carry[0] + over[0] * prod_real + over[1] * prod_imag, carry[1] + over[0] * prod_imag - over[1] * prod_real), None)
    zeros = jnp.zeros(phase.shape, jnp.float32)
    (sum_real, sum_imag), _ = lax.scan(accumulate, (zeros, zeros), (front, back, intersections))
    total_real = sum_real / GRID
    total_imag = sum_imag / GRID
    magnitude = total_real * total_real + total_imag * total_imag
    power_mean = jnp.sum(magnitude) / (GRID * GRID)
    scale_factor = lax.rsqrt(magnitude + 0.25 * power_mean + 1e-06)
    return jnp.stack([total_real * scale_factor, -total_imag * scale_factor]).astype(jnp.bfloat16)

def reference(forward, backward_first, backward_second, phase_first, phase_second):
    tables = make_tables(GRID)
    mask_first = new_mask(forward, backward_first, phase_first)
    mask_real = mask_first[0].astype(jnp.float32)
    mask_imag = mask_first[1].astype(jnp.float32)

    def propagate(front_one):
        front_real = front_one[0].astype(jnp.float32)
        front_imag = front_one[1].astype(jnp.float32)
        field = jnp.stack([front_real * mask_real - front_imag * mask_imag, front_real * mask_imag + front_imag * mask_real]).astype(jnp.bfloat16)[None]
        field = transform(field, tables, True, False)
        field = transform(field, tables, False, False)
        field = transform(field, tables, True, True)
        field = transform(field, tables, False, True)
        return field[0]
    arrived = lax.map(propagate, forward)
    mask_second = new_mask(arrived, backward_second, phase_second)
    return (mask_first, mask_second, arrived)
```

```python
import functools
import math

import jax
import jax.numpy as jnp
import ml_dtypes
import numpy as np
from jax import lax
from jax.experimental import pallas as pl
from jax.experimental.pallas import tpu as pltpu
from jax.sharding import PartitionSpec as P

GRID = 1024
ROWS = 128
MESH = pl.DeviceIdType.MESH
F32 = jnp.float32
BF16 = jnp.bfloat16


@functools.cache
def propagator():
    u = np.arange(GRID)
    turns = u[:, None] * u[None, :] % GRID
    angles = np.minimum(turns, GRID - turns) * (2.0 * math.pi / GRID)
    sign = np.where(turns <= GRID // 2, 1.0, -1.0)
    cosine = np.cos(angles).astype(ml_dtypes.bfloat16).astype(np.float64)
    sine = (sign * np.sin(angles)).astype(ml_dtypes.bfloat16).astype(np.float64)
    f = (u + GRID // 2) % GRID - GRID // 2
    phases = (f * f % (2 * GRID)) * (math.pi / GRID)
    chirp = np.cos(phases) - 1j * np.sin(phases)
    h = ((cosine - 1j * sine) * chirp) @ (cosine + 1j * sine) / GRID
    return np.stack([h.real, h.imag]).astype(ml_dtypes.bfloat16)


def cos_sin(phase):
    x = phase * 0.5
    z = x * x
    s = [(-1.0) ** i / math.factorial(2 * i + 1) for i in range(7)]
    c = [(-1.0) ** i / math.factorial(2 * i) for i in range(7)]
    ps = jnp.full_like(z, s[-1])
    for v in s[-2::-1]:
        ps = ps * z + v
    pc = jnp.full_like(z, c[-1])
    for v in c[-2::-1]:
        pc = pc * z + v
    sn = ps * x
    return 1.0 - 2.0 * sn * sn, 2.0 * sn * pc


def fold(v):
    tiles = [
        v[r : r + 8, c : c + 128] for r in range(0, v.shape[0], 8) for c in range(0, v.shape[1], 128)
    ]
    while len(tiles) > 1:
        tiles = [sum(tiles[i : i + 2]) for i in range(0, len(tiles), 2)]
    return tiles[0]


def kernel(
    f_in, b1_in, b2_in, p1_in, p2_in, h_in, m1_out, m2_out, a_out,
    f, b, ph, h, prod, raw, irecv, wrecv, part, zrecv, full, precv, mask, s, t, g, y, arr,
    ls, ss, rs,
):
    mode = lax.axis_index("mode")
    row = lax.axis_index("row")
    zl = mode // 8
    yc = lax.rem(mode, 8)

    def row_peer(k):
        return (mode, lax.rem(row + k, 8))

    def yc_peer(k):
        return (zl * 8 + lax.rem(yc + k, 8), row)

    def z_peer(k):
        return (lax.rem(zl + k, 8) * 8 + yc, row)

    bar = pltpu.get_barrier_semaphore()

    def greet(k, _):
        for p in (row_peer(k), yc_peer(k), z_peer(k)):
            pl.semaphore_signal(bar, inc=1, device_id=p, device_id_type=MESH)
        return 0

    lax.fori_loop(1, 8, greet, 0)

    loads = [
        pltpu.make_async_copy(src, dst, ls.at[i])
        for i, (src, dst) in enumerate(
            [(f_in, f), (b1_in, b.at[0]), (p1_in, ph.at[0]), (h_in, h), (b2_in, b.at[1]), (p2_in, ph.at[1])]
        )
    ]
    for c in loads:
        c.start()

    class Stage:
        def __init__(self, n, src, dst, peer):
            self.n, self.src, self.dst, self.peer = n, src, dst, peer

        def desc(self, k):
            return pltpu.make_async_remote_copy(
                src_ref=self.src(k), dst_ref=self.dst(k), send_sem=ss.at[self.n, k],
                recv_sem=rs.at[self.n, k], device_id=self.peer(k), device_id_type=MESH,
            )

        def loop(self, what):
            def body(k, _):
                what(self.desc(k))
                return 0

            lax.fori_loop(1, 8, body, 0)

        def start(self):
            self.loop(lambda d: d.start())

        def recv(self):
            self.loop(lambda d: d.wait_recv())

        def sent(self):
            self.loop(lambda d: d.wait_send())

    stages = []

    def stage(*args):
        stages.append(Stage(len(stages), *args))
        return stages[-1]

    def new_mask(i, front, first):
        back, phase = b.at[i], ph.at[i]

        def products(j, acc):
            rows = pl.ds(pl.multiple_of(j * 16, 16), 16)
            fr, fi = front[0, rows, :].astype(F32), front[1, rows, :].astype(F32)
            br, bi = back[0, rows, :].astype(F32), back[1, rows, :].astype(F32)
            pr = br * fr + bi * fi
            pi = br * fi - bi * fr
            prod[i, j, 0] = pr.astype(BF16)
            prod[i, j, 1] = pi.astype(BF16)
            c, sn = cos_sin(phase[rows, :])
            return acc[0] + fold(pr * c - pi * sn), acc[1] + fold(pr * sn + pi * c)

        zero = jnp.zeros((8, 128), F32)
        ir, ii = lax.fori_loop(0, 8, products, (zero, zero))
        irecv[i, 0, 0] = ir
        irecv[i, 0, 1] = ii
        if first:
            pl.semaphore_wait(bar, 21)
        over = stage(lambda k: irecv.at[i, 0], lambda k: irecv.at[i, k], row_peer)
        over.start()
        share = stage(lambda k: prod.at[i, lax.rem(yc + k, 8)], lambda k: raw.at[i, k], yc_peer)
        share.start()
        over.recv()
        for q in range(2):
            wrecv[i, 0, q] = sum(irecv[i, k, q] for k in range(8))
        weight = stage(lambda k: wrecv.at[i, 0], lambda k: wrecv.at[i, k], yc_peer)
        weight.start()
        raw[i, 0] = prod[i, yc]
        share.recv()
        weight.recv()

        def weighted(k, acc):
            wr = jnp.sum(wrecv[i, k, 0], axis=(0, 1), keepdims=True) * (1.0 / GRID)
            wi = jnp.sum(wrecv[i, k, 1], axis=(0, 1), keepdims=True) * (1.0 / GRID)
            pr, pi = raw[i, k, 0].astype(F32), raw[i, k, 1].astype(F32)
            return acc[0] + (wr * pr + wi * pi), acc[1] + (wr * pi - wi * pr)

        zero = jnp.zeros((16, GRID), F32)
        tr, ti = lax.fori_loop(0, 8, weighted, (zero, zero))
        for q in range(8):
            part[i, q, 0] = tr[:, q * 128 : q * 128 + 128].astype(BF16)
            part[i, q, 1] = ti[:, q * 128 : q * 128 + 128].astype(BF16)
        scatter = stage(lambda k: part.at[i, lax.rem(zl + k, 8)], lambda k: zrecv.at[i, k], z_peer)
        scatter.start()
        zrecv[i, 0] = part[i, zl]
        scatter.recv()
        full[i, yc, zl] = sum(zrecv[i, k].astype(F32) for k in range(8)).astype(BF16)
        gather_z = stage(lambda k: full.at[i, yc, zl], lambda k: full.at[i, yc, zl], z_peer)
        gather_z.start()
        gather_z.recv()
        gather_yc = stage(lambda k: full.at[i, yc], lambda k: full.at[i, yc], yc_peer)
        gather_yc.start()
        gather_yc.recv()

        def power(j, acc):
            for q in range(8):
                v = full[i, j, q].astype(F32)
                acc = acc + fold(v[0] * v[0] + v[1] * v[1])
            return acc

        precv[i, 0] = lax.fori_loop(0, 8, power, jnp.zeros((8, 128), F32))
        powers = stage(lambda k: precv.at[i, 0], lambda k: precv.at[i, k], row_peer)
        powers.start()
        powers.recv()
        total = sum(precv[i, k] for k in range(8))
        mean = jnp.sum(total, axis=(0, 1), keepdims=True) * (1.0 / (GRID * GRID))
        floor = 0.25 * mean + 1e-6

        def finish(j, _):
            rows = pl.ds(pl.multiple_of(j * 16, 16), 16)
            for q in range(8):
                v = full[i, j, q].astype(F32)
                scale = lax.rsqrt(v[0] * v[0] + v[1] * v[1] + floor)
                mask[i, 0, rows, q * 128 : q * 128 + 128] = (v[0] * scale).astype(BF16)
                mask[i, 1, rows, q * 128 : q * 128 + 128] = (-v[1] * scale).astype(BF16)
            return 0

        lax.fori_loop(0, 8, finish, 0)

    for c in loads[:3]:
        c.wait()
    new_mask(0, f, True)
    outs = [pltpu.make_async_copy(mask.at[0], m1_out, ls.at[6])]
    outs[0].start()

    def apply(j, _):
        rows = pl.ds(pl.multiple_of(j * 16, 16), 16)
        fr, fi = f[0, rows, :].astype(F32), f[1, rows, :].astype(F32)
        mr, mi = mask[0, 0, rows, :].astype(F32), mask[0, 1, rows, :].astype(F32)
        s[rows, :] = (fr * mr - fi * mi).astype(BF16)
        s[pl.ds(pl.multiple_of(ROWS + j * 16, 16), 16), :] = (fr * mi + fi * mr).astype(BF16)
        return 0

    lax.fori_loop(0, 8, apply, 0)
    for c in loads[3:]:
        c.wait()

    to_cols = stage(
        lambda k: t.at[:, pl.ds(pl.multiple_of(lax.rem(row + k, 8) * 256, 256), 256)],
        lambda k: g.at[pl.ds(pl.multiple_of(row * ROWS, ROWS), ROWS), :],
        row_peer,
    )
    far = 2 * (1 - row // 4)

    def send_to(st, p):
        @pl.when(p != row)
        def _():
            st.desc(lax.rem(p - row + 8, 8)).start()

    def columns(j, _):
        n = lax.rem(far + j, 4)
        cols = pl.ds(pl.multiple_of(n * 256, 256), 256)
        a = jnp.dot(s[...], h[0, :, cols], preferred_element_type=F32)
        c = jnp.dot(s[...], h[1, :, cols], preferred_element_type=F32)
        tr = (a[:ROWS] - c[ROWS:]).astype(BF16)
        ti = (c[:ROWS] + a[ROWS:]).astype(BF16)
        for e in range(2):
            at = n * 512 + e * 256
            t[:, pl.ds(pl.multiple_of(at, 128), 128)] = tr[:, e * 128 : e * 128 + 128]
            t[:, pl.ds(pl.multiple_of(at + 128, 128), 128)] = ti[:, e * 128 : e * 128 + 128]
        for e in range(2):
            send_to(to_cols, 2 * n + e)
        return 0

    lax.fori_loop(0, 4, columns, 0)
    g[pl.ds(pl.multiple_of(row * ROWS, ROWS), ROWS), :] = t[
        :, pl.ds(pl.multiple_of(row * 256, 256), 256)
    ]
    to_cols.recv()

    to_rows = stage(
        lambda k: y.at[lax.rem(row + k, 8)],
        lambda k: arr.at[:, :, pl.ds(pl.multiple_of(row * 128, 128), 128)],
        row_peer,
    )

    def rows_(j, _):
        n = lax.rem(far + j, 4)
        rows = pl.ds(pl.multiple_of(n * 256, 256), 256)
        a = jnp.dot(h[0, rows, :], g[...], preferred_element_type=F32)
        c = jnp.dot(h[1, rows, :], g[...], preferred_element_type=F32)
        yr = (a[:, :128] - c[:, 128:]).astype(BF16)
        yi = (a[:, 128:] + c[:, :128]).astype(BF16)
        for e in range(2):
            y[2 * n + e, 0] = yr[e * ROWS : e * ROWS + ROWS]
            y[2 * n + e, 1] = yi[e * ROWS : e * ROWS + ROWS]
        for e in range(2):
            send_to(to_rows, 2 * n + e)
        return 0

    lax.fori_loop(0, 4, rows_, 0)
    arr[:, :, pl.ds(pl.multiple_of(row * 128, 128), 128)] = y[row]
    to_rows.recv()
    outs.append(pltpu.make_async_copy(arr, a_out, ls.at[7]))
    outs[1].start()
    new_mask(1, arr, False)
    outs.append(pltpu.make_async_copy(mask.at[1], m2_out, ls.at[8]))
    outs[2].start()
    for st in stages:
        st.sent()
    for c in outs:
        c.wait()


def on_device(forward, backward_first, backward_second, phase_first, phase_second):
    hbm = pl.BlockSpec(memory_space=pl.ANY)
    block = (2, ROWS, GRID)
    m1, m2, arrived = pl.pallas_call(
        kernel,
        out_shape=[jax.ShapeDtypeStruct(block, BF16)] * 3,
        in_specs=[hbm] * 6,
        out_specs=[hbm] * 3,
        scratch_shapes=[
            pltpu.VMEM(block, BF16),
            pltpu.VMEM((2, *block), BF16),
            pltpu.VMEM((2, ROWS, GRID), F32),
            pltpu.VMEM((2, GRID, GRID), BF16),
            pltpu.VMEM((2, 8, 2, 16, GRID), BF16),
            pltpu.VMEM((2, 8, 2, 16, GRID), BF16),
            pltpu.VMEM((2, 8, 2, 8, 128), F32),
            pltpu.VMEM((2, 8, 2, 8, 128), F32),
            pltpu.VMEM((2, 8, 2, 16, 128), BF16),
            pltpu.VMEM((2, 8, 2, 16, 128), BF16),
            pltpu.VMEM((2, 8, 8, 2, 16, 128), BF16),
            pltpu.VMEM((2, 8, 8, 128), F32),
            pltpu.VMEM((2, *block), BF16),
            pltpu.VMEM((2 * ROWS, GRID), BF16),
            pltpu.VMEM((ROWS, 2 * GRID), BF16),
            pltpu.VMEM((GRID, 256), BF16),
            pltpu.VMEM((8, 2, ROWS, 128), BF16),
            pltpu.VMEM(block, BF16),
            pltpu.SemaphoreType.DMA((9,)),
            pltpu.SemaphoreType.DMA((16, 8)),
            pltpu.SemaphoreType.DMA((16, 8)),
        ],
        compiler_params=pltpu.CompilerParams(
            collective_id=0, has_side_effects=True, vmem_limit_bytes=40 * 2**20
        ),
    )(
        forward[0], backward_first[0], backward_second[0], phase_first, phase_second,
        jnp.asarray(propagator()),
    )
    return m1, m2, arrived[None]


def solution(mesh):
    in_specs = (
        P("mode", None, "row", None),
        P("mode", None, "row", None),
        P("mode", None, "row", None),
        P("row", None),
        P("row", None),
    )
    out_specs = (P(None, "row", None), P(None, "row", None), P("mode", None, "row", None))
    return jax.shard_map(
        on_device, mesh=mesh, in_specs=in_specs, out_specs=out_specs, check_vma=False
    )
```

```python
import functools
import math

import jax
import jax.numpy as jnp
import ml_dtypes
import numpy as np
from jax import lax
from jax.experimental import pallas as pl
from jax.experimental.pallas import tpu as pltpu
from jax.sharding import PartitionSpec as P

GRID = 1024
ROWS = 128
MESH = pl.DeviceIdType.MESH
F32 = jnp.float32
BF16 = jnp.bfloat16


@functools.cache
def propagator():
    u = np.arange(GRID)
    turns = u[:, None] * u[None, :] % GRID
    angles = np.minimum(turns, GRID - turns) * (2.0 * math.pi / GRID)
    sign = np.where(turns <= GRID // 2, 1.0, -1.0)
    cosine = np.cos(angles).astype(ml_dtypes.bfloat16).astype(np.float64)
    sine = (sign * np.sin(angles)).astype(ml_dtypes.bfloat16).astype(np.float64)
    f = (u + GRID // 2) % GRID - GRID // 2
    phases = (f * f % (2 * GRID)) * (math.pi / GRID)
    chirp = np.cos(phases) - 1j * np.sin(phases)
    h = ((cosine - 1j * sine) * chirp) @ (cosine + 1j * sine) / GRID
    return np.stack([h.real, h.imag]).astype(ml_dtypes.bfloat16)


def cos_sin(phase):
    x = phase * 0.5
    z = x * x
    s = [(-1.0) ** i / math.factorial(2 * i + 1) for i in range(7)]
    c = [(-1.0) ** i / math.factorial(2 * i) for i in range(7)]
    ps = jnp.full_like(z, s[-1])
    for v in s[-2::-1]:
        ps = ps * z + v
    pc = jnp.full_like(z, c[-1])
    for v in c[-2::-1]:
        pc = pc * z + v
    sn = ps * x
    return 1.0 - 2.0 * sn * sn, 2.0 * sn * pc


def fold(v):
    tiles = [
        v[r : r + 8, c : c + 128] for r in range(0, v.shape[0], 8) for c in range(0, v.shape[1], 128)
    ]
    while len(tiles) > 1:
        tiles = [sum(tiles[i : i + 2]) for i in range(0, len(tiles), 2)]
    return tiles[0]


def kernel(
    f_in, b1_in, b2_in, p1_in, p2_in, h_in, m1_out, m2_out, a_out,
    f, b, ph, h, prod, raw, irecv, wrecv, part, zrecv, full, precv, prow, mask, s, t, g, y, arr,
    ls, ss, rs,
):
    mode = lax.axis_index("mode")
    row = lax.axis_index("row")
    zl = mode // 8
    yc = lax.rem(mode, 8)

    def row_peer(k):
        return (mode, lax.rem(row + k, 8))

    def yc_peer(k):
        return (zl * 8 + lax.rem(yc + k, 8), row)

    def z_peer(k):
        return (lax.rem(zl + k, 8) * 8 + yc, row)

    def z16_peer(k):
        z = lax.rem((row // 4) * 8 + zl + k, 16)
        return (lax.rem(z, 8) * 8 + yc, (z // 8) * 4 + lax.rem(row, 4))

    def y_peer(k):
        return (zl * 8 + lax.rem(yc + 2 * (k // 8), 8), row)

    def c_peer(k):
        return (mode + 1 - 2 * lax.rem(mode, 2), row)

    def xyc_peer(k):
        at = lax.rem(lax.rem(row, 4) * 8 + yc + k, 32)
        return (zl * 8 + lax.rem(at, 8), (row // 4) * 4 + at // 8)

    bar = pltpu.get_barrier_semaphore()
    n_greet = 0

    def greet(first, last, peer):
        def body(k, _):
            pl.semaphore_signal(bar, inc=1, device_id=peer(k), device_id_type=MESH)
            return 0

        lax.fori_loop(first, last, body, 0)
        return last - first

    n_greet += greet(1, 8, row_peer)
    n_greet += greet(1, 16, z16_peer)
    n_greet += greet(1, 32, xyc_peer)

    loads = [
        pltpu.make_async_copy(src, dst, ls.at[i])
        for i, (src, dst) in enumerate(
            [(f_in, f), (b1_in, b.at[0]), (p1_in, ph.at[0]), (h_in, h), (b2_in, b.at[1]), (p2_in, ph.at[1])]
        )
    ]
    for c in loads:
        c.start()

    class Stage:
        def __init__(self, n, hi, src, dst, peer, slot=None):
            self.n, self.hi, self.src, self.dst, self.peer = n, hi, src, dst, peer
            self.slot = slot or (lambda k: k)
            self.lo = 8 if peer is y_peer else 1

        def desc(self, k):
            return pltpu.make_async_remote_copy(
                src_ref=self.src(k), dst_ref=self.dst(k), send_sem=ss.at[self.n, k],
                recv_sem=rs.at[self.n, self.slot(k)], device_id=self.peer(k), device_id_type=MESH,
            )

        def loop(self, what):
            def body(k, _):
                what(self.desc(k))
                return 0

            lax.fori_loop(self.lo, self.hi, body, 0)

        def start(self):
            self.loop(lambda d: d.start())

        def recv(self):
            self.loop(lambda d: d.wait_recv())

        def sent(self):
            self.loop(lambda d: d.wait_send())

    stages = []

    def stage(*args):
        stages.append(Stage(len(stages), *args))
        return stages[-1]

    def new_mask(i, front, first):
        back, phase = b.at[i], ph.at[i]

        def products(j, acc):
            rows = pl.ds(pl.multiple_of(j * 16, 16), 16)
            fr, fi = front[0, rows, :].astype(F32), front[1, rows, :].astype(F32)
            br, bi = back[0, rows, :].astype(F32), back[1, rows, :].astype(F32)
            pr = br * fr + bi * fi
            pi = br * fi - bi * fr
            for q in range(8):
                prod[i, j, q, 0] = pr[:, q * 128 : q * 128 + 128].astype(BF16)
                prod[i, j, q, 1] = pi[:, q * 128 : q * 128 + 128].astype(BF16)
            c, sn = cos_sin(phase[rows, :])
            return acc[0] + fold(pr * c - pi * sn), acc[1] + fold(pr * sn + pi * c)

        zero = jnp.zeros((8, 128), F32)
        ir, ii = lax.fori_loop(0, 8, products, (zero, zero))
        irecv[i, 0, 0] = jnp.sum(ir, axis=0, keepdims=True)
        irecv[i, 0, 1] = jnp.sum(ii, axis=0, keepdims=True)
        if first:
            pl.semaphore_wait(bar, n_greet)
        over = stage(8, lambda k: irecv.at[i, 0], lambda k: irecv.at[i, k], row_peer)
        over.start()
        share = stage(8, lambda k: prod.at[i, lax.rem(yc + k, 8)], lambda k: raw.at[i, k], yc_peer)
        share.start()
        over.recv()
        for q in range(2):
            wrecv[i, 0, q] = sum(irecv[i, k, q] for k in range(8))
        weight = stage(8, lambda k: wrecv.at[i, 0], lambda k: wrecv.at[i, k], yc_peer)
        weight.start()
        raw[i, 0] = prod[i, yc]
        share.recv()
        weight.recv()
        weights = [
            [jnp.sum(wrecv[i, k, q], axis=1, keepdims=True) * (1.0 / GRID) for q in range(2)]
            for k in range(8)
        ]

        scatter = stage(8, lambda k: part.at[i, k], lambda k: zrecv.at[i, k], z_peer)

        def weighted(k, _):
            q = lax.rem(zl + k, 8)
            tr = jnp.zeros((16, 128), F32)
            ti = jnp.zeros((16, 128), F32)
            for m in range(8):
                pr, pi = raw[i, m, q, 0].astype(F32), raw[i, m, q, 1].astype(F32)
                wr, wi = weights[m]
                tr = tr + (wr * pr + wi * pi)
                ti = ti + (wr * pi - wi * pr)
            part[i, k, 0] = tr.astype(BF16)
            part[i, k, 1] = ti.astype(BF16)

            @pl.when(k < 8)
            def _():
                scatter.desc(k).start()

            return 0

        lax.fori_loop(1, 9, weighted, 0)
        zrecv[i, 0] = part[i, 8]
        scatter.recv()
        piece = sum(zrecv[i, k].astype(F32) for k in range(8)).astype(BF16)
        full[i, yc, zl] = piece
        gather_z = stage(
            8, lambda k: full.at[i, yc, zl], lambda k: full.at[i, yc, zl], z_peer, lambda k: zl
        )
        gather_z.start()
        v = piece.astype(F32)
        precv[i, 0] = jnp.sum(fold(v[0] * v[0] + v[1] * v[1]), axis=0, keepdims=True)
        power_z = stage(16, lambda k: precv.at[i, 0], lambda k: precv.at[i, k], z16_peer)
        power_z.start()

        gather_y = stage(32, lambda k: full.at[i, yc, k % 8], lambda k: full.at[i, yc, k % 8], y_peer)

        def onward(q):
            for o in (1, 2, 3):
                gather_y.desc(o * 8 + q).start()

        onward(zl)

        def forward_z(d, _):
            for q in (zl - d, zl + d):

                @pl.when((q >= 0) & (q < 8))
                def _():
                    pltpu.make_async_remote_copy(
                        src_ref=full.at[i, yc, zl], dst_ref=full.at[i, yc, q],
                        send_sem=ss.at[gather_z.n, 0], recv_sem=rs.at[gather_z.n, q],
                        device_id=z_peer(1), device_id_type=MESH,
                    ).wait_recv()
                    onward(q)

            return 0

        lax.fori_loop(1, 8, forward_z, 0)
        gather_c = stage(
            5, lambda k: full.at[i, lax.rem(yc + 2 * k, 8)], lambda k: full.at[i, lax.rem(yc + 2 * k, 8)], c_peer
        )
        gather_c.desc(4).start()
        power_z.recv()
        prow[i, 0] = sum(precv[i, k] for k in range(16))
        power_xy = stage(32, lambda k: prow.at[i, 0], lambda k: prow.at[i, k], xyc_peer)
        power_xy.start()

        def forward_y(o, _):
            def wait(q, _):
                gather_y.desc(o * 8 + q).wait_recv()
                return 0

            lax.fori_loop(0, 8, wait, 0)
            gather_c.desc(4 - o).start()
            return 0

        lax.fori_loop(1, 4, forward_y, 0)
        power_xy.recv()
        total = sum(prow[i, k] for k in range(32))
        mean = jnp.sum(total, axis=1, keepdims=True) * (1.0 / (GRID * GRID))
        floor = 0.25 * mean + 1e-6
        gather_c.recv()

        def finish(j, _):
            rows = pl.ds(pl.multiple_of(j * 16, 16), 16)
            for q in range(8):
                v = full[i, j, q].astype(F32)
                scale = lax.rsqrt(v[0] * v[0] + v[1] * v[1] + floor)
                mask[i, 0, rows, q * 128 : q * 128 + 128] = (v[0] * scale).astype(BF16)
                mask[i, 1, rows, q * 128 : q * 128 + 128] = (-v[1] * scale).astype(BF16)
            return 0

        lax.fori_loop(0, 8, finish, 0)
    for c in loads[:3]:
        c.wait()
    new_mask(0, f, True)
    outs = [pltpu.make_async_copy(mask.at[0], m1_out, ls.at[6])]
    outs[0].start()

    def apply(j, _):
        rows = pl.ds(pl.multiple_of(j * 16, 16), 16)
        fr, fi = f[0, rows, :].astype(F32), f[1, rows, :].astype(F32)
        mr, mi = mask[0, 0, rows, :].astype(F32), mask[0, 1, rows, :].astype(F32)
        s[rows, :] = (fr * mr - fi * mi).astype(BF16)
        s[pl.ds(pl.multiple_of(ROWS + j * 16, 16), 16), :] = (fr * mi + fi * mr).astype(BF16)
        return 0

    lax.fori_loop(0, 8, apply, 0)
    for c in loads[3:]:
        c.wait()

    to_cols = stage(
        8,
        lambda k: t.at[:, pl.ds(pl.multiple_of(lax.rem(row + k, 8) * 256, 256), 256)],
        lambda k: g.at[pl.ds(pl.multiple_of(row * ROWS, ROWS), ROWS), :],
        row_peer,
    )
    far = 2 * (1 - row // 4)

    def send_to(st, p):
        @pl.when(p != row)
        def _():
            st.desc(lax.rem(p - row + 8, 8)).start()

    def columns(j, _):
        n = lax.rem(far + j, 4)
        cols = pl.ds(pl.multiple_of(n * 256, 256), 256)
        a = jnp.dot(s[...], h[0, :, cols], preferred_element_type=F32)
        c = jnp.dot(s[...], h[1, :, cols], preferred_element_type=F32)
        tr = (a[:ROWS] - c[ROWS:]).astype(BF16)
        ti = (c[:ROWS] + a[ROWS:]).astype(BF16)
        for e in range(2):
            at = n * 512 + e * 256
            t[:, pl.ds(pl.multiple_of(at, 128), 128)] = tr[:, e * 128 : e * 128 + 128]
            t[:, pl.ds(pl.multiple_of(at + 128, 128), 128)] = ti[:, e * 128 : e * 128 + 128]
        for e in range(2):
            send_to(to_cols, 2 * n + e)
        return 0

    lax.fori_loop(0, 4, columns, 0)
    g[pl.ds(pl.multiple_of(row * ROWS, ROWS), ROWS), :] = t[
        :, pl.ds(pl.multiple_of(row * 256, 256), 256)
    ]
    to_cols.recv()

    to_rows = stage(
        8,
        lambda k: y.at[lax.rem(row + k, 8)],
        lambda k: arr.at[:, :, pl.ds(pl.multiple_of(row * 128, 128), 128)],
        row_peer,
    )

    def rows_(j, _):
        n = lax.rem(far + j, 4)
        rows = pl.ds(pl.multiple_of(n * 256, 256), 256)
        a = jnp.dot(h[0, rows, :], g[...], preferred_element_type=F32)
        c = jnp.dot(h[1, rows, :], g[...], preferred_element_type=F32)
        yr = (a[:, :128] - c[:, 128:]).astype(BF16)
        yi = (a[:, 128:] + c[:, :128]).astype(BF16)
        for e in range(2):
            y[2 * n + e, 0] = yr[e * ROWS : e * ROWS + ROWS]
            y[2 * n + e, 1] = yi[e * ROWS : e * ROWS + ROWS]
        for e in range(2):
            send_to(to_rows, 2 * n + e)
        return 0

    lax.fori_loop(0, 4, rows_, 0)
    arr[:, :, pl.ds(pl.multiple_of(row * 128, 128), 128)] = y[row]
    to_rows.recv()
    outs.append(pltpu.make_async_copy(arr, a_out, ls.at[7]))
    outs[1].start()
    new_mask(1, arr, False)
    outs.append(pltpu.make_async_copy(mask.at[1], m2_out, ls.at[8]))
    outs[2].start()
    for st in stages:
        st.sent()
    for c in outs:
        c.wait()


def on_device(forward, backward_first, backward_second, phase_first, phase_second):
    hbm = pl.BlockSpec(memory_space=pl.ANY)
    block = (2, ROWS, GRID)
    m1, m2, arrived = pl.pallas_call(
        kernel,
        out_shape=[jax.ShapeDtypeStruct(block, BF16)] * 3,
        in_specs=[hbm] * 6,
        out_specs=[hbm] * 3,
        scratch_shapes=[
            pltpu.VMEM(block, BF16),
            pltpu.VMEM((2, *block), BF16),
            pltpu.VMEM((2, ROWS, GRID), F32),
            pltpu.VMEM((2, GRID, GRID), BF16),
            pltpu.VMEM((2, 8, 8, 2, 16, 128), BF16),
            pltpu.VMEM((2, 8, 8, 2, 16, 128), BF16),
            pltpu.VMEM((2, 8, 2, 1, 128), F32),
            pltpu.VMEM((2, 8, 2, 1, 128), F32),
            pltpu.VMEM((2, 9, 2, 16, 128), BF16),
            pltpu.VMEM((2, 8, 2, 16, 128), BF16),
            pltpu.VMEM((2, 8, 8, 2, 16, 128), BF16),
            pltpu.VMEM((2, 16, 1, 128), F32),
            pltpu.VMEM((2, 32, 1, 128), F32),
            pltpu.VMEM((2, *block), BF16),
            pltpu.VMEM((2 * ROWS, GRID), BF16),
            pltpu.VMEM((ROWS, 2 * GRID), BF16),
            pltpu.VMEM((GRID, 256), BF16),
            pltpu.VMEM((8, 2, ROWS, 128), BF16),
            pltpu.VMEM(block, BF16),
            pltpu.SemaphoreType.DMA((9,)),
            pltpu.SemaphoreType.DMA((20, 32)),
            pltpu.SemaphoreType.DMA((20, 32)),
        ],
        compiler_params=pltpu.CompilerParams(
            collective_id=0, has_side_effects=True, vmem_limit_bytes=60 * 2**20
        ),
    )(
        forward[0], backward_first[0], backward_second[0], phase_first, phase_second,
        jnp.asarray(propagator()),
    )
    return m1, m2, arrived[None]


def solution(mesh):
    in_specs = (
        P("mode", None, "row", None),
        P("mode", None, "row", None),
        P("mode", None, "row", None),
        P("row", None),
        P("row", None),
    )
    out_specs = (P(None, "row", None), P(None, "row", None), P("mode", None, "row", None))
    return jax.shard_map(
        on_device, mesh=mesh, in_specs=in_specs, out_specs=out_specs, check_vma=False
    )
```

```python
import functools
import math

import jax
import jax.numpy as jnp
import ml_dtypes
import numpy as np
from jax import lax
from jax.experimental import pallas as pl
from jax.experimental.pallas import tpu as pltpu
from jax.sharding import PartitionSpec as P

GRID = 1024
ROWS = 128
MESH = pl.DeviceIdType.MESH
F32 = jnp.float32
BF16 = jnp.bfloat16


@functools.cache
def propagator():
    u = np.arange(GRID)
    turns = u[:, None] * u[None, :] % GRID
    angles = np.minimum(turns, GRID - turns) * (2.0 * math.pi / GRID)
    sign = np.where(turns <= GRID // 2, 1.0, -1.0)
    cosine = np.cos(angles).astype(ml_dtypes.bfloat16).astype(np.float64)
    sine = (sign * np.sin(angles)).astype(ml_dtypes.bfloat16).astype(np.float64)
    f = (u + GRID // 2) % GRID - GRID // 2
    phases = (f * f % (2 * GRID)) * (math.pi / GRID)
    chirp = np.cos(phases) - 1j * np.sin(phases)
    h = ((cosine - 1j * sine) * chirp) @ (cosine + 1j * sine) / GRID
    return np.stack([h.real, h.imag]).astype(ml_dtypes.bfloat16)


def cos_sin(phase):
    x = phase * 0.5
    z = x * x
    s = [(-1.0) ** i / math.factorial(2 * i + 1) for i in range(7)]
    c = [(-1.0) ** i / math.factorial(2 * i) for i in range(7)]
    ps = jnp.full_like(z, s[-1])
    for v in s[-2::-1]:
        ps = ps * z + v
    pc = jnp.full_like(z, c[-1])
    for v in c[-2::-1]:
        pc = pc * z + v
    sn = ps * x
    return 1.0 - 2.0 * sn * sn, 2.0 * sn * pc


def fold(v):
    tiles = [
        v[r : r + 8, c : c + 128] for r in range(0, v.shape[0], 8) for c in range(0, v.shape[1], 128)
    ]
    while len(tiles) > 1:
        tiles = [sum(tiles[i : i + 2]) for i in range(0, len(tiles), 2)]
    return tiles[0]


def kernel(
    f_in, b1_in, b2_in, p1_in, p2_in, h_in, m1_out, m2_out, a_out,
    f, b, ph, h, raws, px, prod, raw, irecv, wrecv, part, zrecv, precv, prow,
    both, full, m1, m1recv, mask, g, yb, s, arr, ls, ss, rs,
):
    mode = lax.axis_index("mode")
    row = lax.axis_index("row")
    zl, yc = mode // 8, lax.rem(mode, 8)
    zh, x = row // 4, lax.rem(row, 4)

    def row_peer(k):
        return (mode, lax.rem(row + k, 8))

    def x_peer(k):
        return (mode, zh * 4 + lax.rem(x + k, 4))

    def yc_peer(k):
        return (zl * 8 + lax.rem(yc + k, 8), row)

    def z_peer(k):
        return (lax.rem(zl + k, 8) * 8 + yc, row)

    def z16_peer(k):
        z = lax.rem(zh * 8 + zl + k, 16)
        return (lax.rem(z, 8) * 8 + yc, (z // 8) * 4 + x)

    def y_peer(k):
        return (zl * 8 + lax.rem(yc + 2 * k, 8), row)

    def c_peer(k):
        return (mode + 1 - 2 * lax.rem(mode, 2), row)

    def xyc_peer(k):
        at = lax.rem(x * 8 + yc + k, 32)
        return (zl * 8 + lax.rem(at, 8), zh * 4 + at // 8)

    bar = pltpu.get_barrier_semaphore()

    def greet(last, peer):
        def body(k, _):
            pl.semaphore_signal(bar, inc=1, device_id=peer(k), device_id_type=MESH)
            return 0

        lax.fori_loop(1, last, body, 0)

    greet(8, row_peer)
    greet(16, z16_peer)
    greet(32, xyc_peer)

    loads = [
        pltpu.make_async_copy(src, dst, ls.at[i])
        for i, (src, dst) in enumerate(
            [(f_in, f), (b1_in, b.at[0]), (p1_in, ph.at[0]), (h_in, h), (b2_in, b.at[1]), (p2_in, ph.at[1])]
        )
    ]
    for c in loads:
        c.start()

    used = [0, 0]
    sent = []

    class Stage:
        def __init__(self, src, dst, peer, all_sent, all_came=None, came=1):
            self.src, self.dst, self.peer, self.all_came = src, dst, peer, all_came
            self.s, self.r = used
            used[0] += 1
            used[1] += came
            sent.append(lambda: self.desc(0, 0, all_sent).wait_send())

        def desc(self, k, slot=0, whole=None):
            return pltpu.make_async_remote_copy(
                src_ref=self.src(k) if whole is None else whole,
                dst_ref=self.dst(k) if whole is None else whole,
                send_sem=ss.at[self.s], recv_sem=rs.at[self.r + slot],
                device_id=self.peer(1), device_id_type=MESH,
            )

        def start(self, k, slot=0):
            pltpu.make_async_remote_copy(
                src_ref=self.src(k), dst_ref=self.dst(k), send_sem=ss.at[self.s],
                recv_sem=rs.at[self.r + slot], device_id=self.peer(k), device_id_type=MESH,
            ).start()

        def start_all(self, last, first=1):
            def body(k, _):
                self.start(k)
                return 0

            lax.fori_loop(first, last, body, 0)

        def wait(self, whole=None, slot=0):
            self.desc(0, slot, self.all_came if whole is None else whole).wait_recv()

    def sixteen(j):
        return pl.ds(pl.multiple_of(j * 16, 16), 16)

    def products(i, front, put):
        back, phase = b.at[i], ph.at[i]

        def body(j, acc):
            rows = sixteen(j)
            fr, fi = front[0, rows, :].astype(F32), front[1, rows, :].astype(F32)
            br, bi = back[0, rows, :].astype(F32), back[1, rows, :].astype(F32)
            pr = br * fr + bi * fi
            pi = br * fi - bi * fr
            for q in range(8):
                cols = slice(q * 128, q * 128 + 128)
                put(j, q, jnp.stack([pr[:, cols], pi[:, cols]]).astype(BF16))
            c, sn = cos_sin(phase[rows, :])
            return acc[0] + fold(pr * c - pi * sn), acc[1] + fold(pr * sn + pi * c)

        zero = jnp.zeros((8, 128), F32)
        ir, ii = lax.fori_loop(0, 8, body, (zero, zero))
        irecv[i, 0, 0] = jnp.sum(ir, axis=0, keepdims=True)
        irecv[i, 0, 1] = jnp.sum(ii, axis=0, keepdims=True)

    def overlap(i):
        st = Stage(
            lambda k: irecv.at[i, 0], lambda k: irecv.at[i, k], row_peer,
            irecv.at[i, pl.ds(1, 7)], irecv.at[i, pl.ds(1, 7)],
        )
        st.start_all(8)
        return st

    def share_products(i):
        st = Stage(
            lambda k: prod.at[i, lax.rem(yc + k, 8)], lambda k: raw.at[i, k], yc_peer,
            raw.at[i, pl.ds(1, 7)], raw.at[i, pl.ds(1, 7)],
        )
        st.start_all(8)
        return st

    def share_weights(i):
        for q in range(2):
            wrecv[i, 0, q] = sum(irecv[i, k, q] for k in range(8))
        st = Stage(
            lambda k: wrecv.at[i, 0], lambda k: wrecv.at[i, k], yc_peer,
            wrecv.at[i, pl.ds(1, 7)], wrecv.at[i, pl.ds(1, 7)],
        )
        st.start_all(8)
        return st

    def reduced(i):
        weights = [
            [jnp.sum(wrecv[i, k, q], axis=1, keepdims=True) * (1.0 / GRID) for q in range(2)]
            for k in range(8)
        ]
        st = Stage(
            lambda k: part.at[i, k], lambda k: zrecv.at[i, k], z_peer,
            zrecv.at[i, pl.ds(1, 7)], zrecv.at[i, pl.ds(1, 7)],
        )

        def body(k, _):
            q = lax.rem(zl + k, 8)
            tr = jnp.zeros((16, 128), F32)
            ti = jnp.zeros((16, 128), F32)
            for m in range(8):
                pr, pi = raw[i, m, q, 0].astype(F32), raw[i, m, q, 1].astype(F32)
                wr, wi = weights[m]
                tr = tr + (wr * pr + wi * pi)
                ti = ti + (wr * pi - wi * pr)
            part[i, k, 0] = tr.astype(BF16)
            part[i, k, 1] = ti.astype(BF16)

            @pl.when(k < 8)
            def _():
                st.start(k)

            return 0

        lax.fori_loop(1, 9, body, 0)
        zrecv[i, 0] = part[i, 8]
        st.wait()
        return sum(zrecv[i, k].astype(F32) for k in range(8)).astype(BF16)

    def power_z(i, piece):
        v = piece.astype(F32)
        precv[i, 0] = jnp.sum(fold(v[0] * v[0] + v[1] * v[1]), axis=0, keepdims=True)
        st = Stage(
            lambda k: precv.at[i, 0], lambda k: precv.at[i, k], z16_peer,
            precv.at[i, pl.ds(1, 15)], precv.at[i, pl.ds(1, 15)],
        )
        st.start_all(16)
        return st

    def power_xy(i):
        prow[i, 0] = sum(precv[i, k] for k in range(16))
        st = Stage(
            lambda k: prow.at[i, 0], lambda k: prow.at[i, k], xyc_peer,
            prow.at[i, pl.ds(1, 31)], prow.at[i, pl.ds(1, 31)],
        )
        st.start_all(32)
        return st

    def power_floor(i):
        total = sum(prow[i, k] for k in range(32))
        mean = jnp.sum(total, axis=1, keepdims=True) * (1.0 / (GRID * GRID))
        return 0.25 * mean + 1e-6

    def masked(piece, floor):
        v = piece.astype(F32)
        scale = lax.rsqrt(v[0] * v[0] + v[1] * v[1] + floor)
        return (v[0] * scale).astype(BF16), (-v[1] * scale).astype(BF16)

    for c in loads[:3]:
        c.wait()

    def put_first(j, q, pair):
        px[q // 2, j // 4, lax.rem(j, 4) * 2 + q % 2] = pair

    products(0, f, put_first)
    pl.semaphore_wait(bar, 7 + 15 + 31)
    over = overlap(0)
    turn = Stage(
        lambda k: px.at[lax.rem(x + k, 4)], lambda k: prod.at[0, pl.ds(2 * x, 2)], x_peer,
        prod.at[0, pl.ds(0, 6)], prod.at[0, pl.ds(0, 6)],
    )
    turn.start_all(4)

    def block(r, half):
        return pl.ds(pl.multiple_of(lax.rem(r, 4) * 256 + half * 128, 128), 128)

    moves = []
    for half in range(2):
        st = Stage(
            lambda k, half=half: f.at[:, :, block(row + k, half)],
            lambda k, half=half: raws.at[half, row], row_peer,
            raws.at[half, pl.ds(0, 7)], raws.at[half, pl.ds(0, 7)],
        )
        moves.append(st)

    def far(k):
        return (lax.rem(row + k, 8) // 4) != zh

    def move(half, want_far):
        def body(k, _):
            @pl.when(far(k) if want_far else jnp.logical_not(far(k)))
            def _():
                moves[half].start(k)

            return 0

        lax.fori_loop(1, 8, body, 0)

    move(0, True)
    move(1, True)
    own = [
        pltpu.make_async_copy(f.at[:, :, block(row, half)], raws.at[half, row], ls.at[9 + half])
        for half in range(2)
    ]
    for c in own:
        c.start()
    prod[0, pl.ds(2 * x, 2)] = px[x]
    turn.wait()
    share = share_products(0)
    move(0, False)
    move(1, False)
    over.wait()
    weight = share_weights(0)
    raw[0, 0] = prod[0, yc]
    share.wait()
    weight.wait()
    piece = reduced(0)
    both[yc, 2 * zl + zh] = piece
    gather_z = Stage(
        lambda k: both.at[yc, 2 * zl + zh], lambda k: both.at[yc, 2 * zl + zh], z16_peer,
        both.at[yc, pl.ds(0, 15)], both.at[yc, pl.ds(0, 15)],
    )
    gather_z.start_all(16)
    pz = power_z(0, piece)
    gather_z.wait()
    gather_y = Stage(
        lambda k: both.at[yc], lambda k: both.at[yc], y_peer, both.at[pl.ds(0, 3)], None, 3
    )
    for o in range(1, 4):
        gather_y.start(o, o - 1)
    gather_c = Stage(
        lambda k: both.at[lax.rem(yc + 2 * k, 8)], lambda k: both.at[lax.rem(yc + 2 * k, 8)], c_peer,
        both.at[pl.ds(0, 4)], both.at[pl.ds(0, 4)],
    )
    gather_c.start(4)
    pz.wait()
    pxy = power_xy(0)
    for o in range(1, 4):
        gather_y.wait(both.at[0], o - 1)
        gather_c.start(4 - o)
    pxy.wait()
    floor = power_floor(0)
    gather_c.wait()
    for c in own:
        c.wait()
    for c in loads[3:]:
        c.wait()

    to_rows = []
    for half in range(2):
        moves[half].wait()

        def apply(j, _, half=half):
            z, n = j // 8, lax.rem(j, 8)
            for u in range(4):
                mr, mi = masked(both[n, (2 * u + half) * 2 + z], floor)
                at = lax.rem(n, 2) * 64 + u * 16

                @pl.when(z == zh)
                def _():
                    m1[n, 2 * u + half, 0] = mr
                    m1[n, 2 * u + half, 1] = mi

                rows = pl.ds(pl.multiple_of(at, 16), 16)
                fr = raws[half, z * 4 + n // 2, 0, rows, :].astype(F32)
                fi = raws[half, z * 4 + n // 2, 1, rows, :].astype(F32)
                mr, mi = mr.astype(F32), mi.astype(F32)
                rows = pl.ds(pl.multiple_of(j * 64 + u * 16, 16), 16)
                g[half, rows, 0:128] = (fr * mr - fi * mi).astype(BF16)
                g[half, rows, 128:256] = (fr * mi + fi * mr).astype(BF16)
            return 0

        lax.fori_loop(0, 16, apply, 0)
        st = Stage(
            lambda k, half=half: yb.at[half, lax.rem(x + k, 4)],
            lambda k, half=half: s.at[:, :, pl.ds(pl.multiple_of(x * 256 + half * 128, 128), 128)],
            x_peer, yb.at[half, pl.ds(0, 3)], yb.at[half, pl.ds(0, 3)],
        )
        to_rows.append(st)
        for n in range(2):
            rows = pl.ds(pl.multiple_of(zh * 512 + n * 256, 256), 256)
            a = jnp.dot(h[0, rows, :], g[half], preferred_element_type=F32)
            c = jnp.dot(h[1, rows, :], g[half], preferred_element_type=F32)
            yr = (a[:, :128] - c[:, 128:]).astype(BF16)
            yi = (a[:, 128:] + c[:, :128]).astype(BF16)
            for e in range(2):
                to = 2 * n + e
                yb[half, to, 0] = yr[e * ROWS : e * ROWS + ROWS]
                yb[half, to, 1] = yi[e * ROWS : e * ROWS + ROWS]

                @pl.when(to != x)
                def _(to=to, st=st):
                    st.start(lax.rem(to - x + 4, 4))

        s[:, :, pl.ds(pl.multiple_of(x * 256 + half * 128, 128), 128)] = yb[half, x]

    for half in range(2):
        to_rows[half].wait()

    def columns(n, _):
        cols = pl.ds(pl.multiple_of(n * 256, 256), 256)
        field = s[...].reshape(2 * ROWS, GRID)
        a = jnp.dot(field, h[0, :, cols], preferred_element_type=F32)
        c = jnp.dot(field, h[1, :, cols], preferred_element_type=F32)
        arr[0, :, cols] = (a[:ROWS] - c[ROWS:]).astype(BF16)
        arr[1, :, cols] = (c[:ROWS] + a[ROWS:]).astype(BF16)
        return 0

    lax.fori_loop(0, 4, columns, 0)
    outs = [pltpu.make_async_copy(arr, a_out, ls.at[6])]
    outs[0].start()

    def put_second(j, q, pair):
        prod[1, j, q] = pair

    products(1, arr, put_second)
    over = overlap(1)
    share = share_products(1)
    back1 = Stage(
        lambda k: m1.at[pl.ds(2 * lax.rem(x + k, 4), 2)], lambda k: m1recv.at[x], x_peer,
        m1recv.at[pl.ds(0, 3)], m1recv.at[pl.ds(0, 3)],
    )
    back1.start_all(4)
    m1recv[x] = m1[pl.ds(2 * x, 2)]
    over.wait()
    weight = share_weights(1)
    raw[1, 0] = prod[1, yc]
    share.wait()
    weight.wait()
    piece = reduced(1)
    full[yc, zl] = piece
    gather_z = Stage(
        lambda k: full.at[yc, zl], lambda k: full.at[yc, zl], z_peer, full.at[yc, pl.ds(0, 7)], None, 8
    )

    def spread(k, _):
        gather_z.start(k, zl)
        return 0

    lax.fori_loop(1, 8, spread, 0)
    pz = power_z(1, piece)

    gather_y2 = [
        Stage(lambda q: full.at[yc, q], lambda q: full.at[yc, q], lambda k, o=o: y_peer(o), full.at[yc], full.at[0])
        for o in range(1, 4)
    ]

    def onward(q):
        for st in gather_y2:
            st.start(q)

    onward(zl)

    def forward(d, _):
        for q in (zl - d, zl + d):

            @pl.when((q >= 0) & (q < 8))
            def _():
                gather_z.wait(full.at[yc, q], q)
                onward(q)

        return 0

    lax.fori_loop(1, 8, forward, 0)
    gather_c = Stage(
        lambda k: full.at[lax.rem(yc + 2 * k, 8)], lambda k: full.at[lax.rem(yc + 2 * k, 8)], c_peer,
        full.at[pl.ds(0, 4)], full.at[pl.ds(0, 4)],
    )
    gather_c.start(4)
    pz.wait()
    pxy = power_xy(1)
    for o in range(1, 4):
        gather_y2[o - 1].wait()
        gather_c.start(4 - o)

    back1.wait()

    def lay(j, _):
        for q in range(8):
            v = m1recv[q // 2, j // 4, lax.rem(j, 4) * 2 + q % 2]
            mask[0, 0, sixteen(j), q * 128 : q * 128 + 128] = v[0]
            mask[0, 1, sixteen(j), q * 128 : q * 128 + 128] = v[1]
        return 0

    lax.fori_loop(0, 8, lay, 0)
    outs.append(pltpu.make_async_copy(mask.at[0], m1_out, ls.at[7]))
    outs[1].start()
    pxy.wait()
    floor2 = power_floor(1)
    gather_c.wait()

    def finish(j, _):
        for q in range(8):
            mr, mi = masked(full[j, q], floor2)
            mask[1, 0, sixteen(j), q * 128 : q * 128 + 128] = mr
            mask[1, 1, sixteen(j), q * 128 : q * 128 + 128] = mi
        return 0

    lax.fori_loop(0, 8, finish, 0)
    outs.append(pltpu.make_async_copy(mask.at[1], m2_out, ls.at[8]))
    outs[2].start()
    for w in sent:
        w()
    for c in outs:
        c.wait()


def on_device(forward, backward_first, backward_second, phase_first, phase_second):
    hbm = pl.BlockSpec(memory_space=pl.ANY)
    block = (2, ROWS, GRID)
    tile = (2, 16, 128)
    m1, m2, arrived = pl.pallas_call(
        kernel,
        out_shape=[jax.ShapeDtypeStruct(block, BF16)] * 3,
        in_specs=[hbm] * 6,
        out_specs=[hbm] * 3,
        scratch_shapes=[
            pltpu.VMEM(block, BF16),
            pltpu.VMEM((2, *block), BF16),
            pltpu.VMEM((2, ROWS, GRID), F32),
            pltpu.VMEM((2, GRID, GRID), BF16),
            pltpu.VMEM((2, 8, 2, ROWS, 128), BF16),
            pltpu.VMEM((4, 2, 8, *tile), BF16),
            pltpu.VMEM((2, 8, 8, *tile), BF16),
            pltpu.VMEM((2, 8, 8, *tile), BF16),
            pltpu.VMEM((2, 8, 2, 1, 128), F32),
            pltpu.VMEM((2, 8, 2, 1, 128), F32),
            pltpu.VMEM((2, 9, *tile), BF16),
            pltpu.VMEM((2, 8, *tile), BF16),
            pltpu.VMEM((2, 16, 1, 128), F32),
            pltpu.VMEM((2, 32, 1, 128), F32),
            pltpu.VMEM((8, 16, *tile), BF16),
            pltpu.VMEM((8, 8, *tile), BF16),
            pltpu.VMEM((8, 8, *tile), BF16),
            pltpu.VMEM((4, 2, 8, *tile), BF16),
            pltpu.VMEM((2, *block), BF16),
            pltpu.VMEM((2, GRID, 256), BF16),
            pltpu.VMEM((2, 4, 2, ROWS, 128), BF16),
            pltpu.VMEM(block, BF16),
            pltpu.VMEM(block, BF16),
            pltpu.SemaphoreType.DMA((11,)),
            pltpu.SemaphoreType.DMA((32,)),
            pltpu.SemaphoreType.DMA((40,)),
        ],
        compiler_params=pltpu.CompilerParams(
            collective_id=0, has_side_effects=True, vmem_limit_bytes=60 * 2**20
        ),
    )(
        forward[0], backward_first[0], backward_second[0], phase_first, phase_second,
        jnp.asarray(propagator()),
    )
    return m1, m2, arrived[None]


def solution(mesh):
    in_specs = (
        P("mode", None, "row", None),
        P("mode", None, "row", None),
        P("mode", None, "row", None),
        P("row", None),
        P("row", None),
    )
    out_specs = (P(None, "row", None), P(None, "row", None), P("mode", None, "row", None))
    return jax.shard_map(
        on_device, mesh=mesh, in_specs=in_specs, out_specs=out_specs, check_vma=False
    )
```

```python
import functools
import math

import jax
import jax.numpy as jnp
import ml_dtypes
import numpy as np
from jax import lax
from jax.experimental import pallas as pl
from jax.experimental.pallas import tpu as pltpu
from jax.sharding import PartitionSpec as P

GRID = 1024
ROWS = 128
MESH = pl.DeviceIdType.MESH
F32 = jnp.float32
BF16 = jnp.bfloat16


@functools.cache
def propagator():
    u = np.arange(GRID)
    turns = u[:, None] * u[None, :] % GRID
    angles = np.minimum(turns, GRID - turns) * (2.0 * math.pi / GRID)
    sign = np.where(turns <= GRID // 2, 1.0, -1.0)
    cosine = np.cos(angles).astype(ml_dtypes.bfloat16).astype(np.float64)
    sine = (sign * np.sin(angles)).astype(ml_dtypes.bfloat16).astype(np.float64)
    f = (u + GRID // 2) % GRID - GRID // 2
    phases = (f * f % (2 * GRID)) * (math.pi / GRID)
    chirp = np.cos(phases) - 1j * np.sin(phases)
    h = ((cosine - 1j * sine) * chirp) @ (cosine + 1j * sine) / GRID
    return np.stack([h.real, h.imag]).astype(ml_dtypes.bfloat16)


def cos_sin(phase):
    x = phase * 0.5
    z = x * x
    s = [(-1.0) ** i / math.factorial(2 * i + 1) for i in range(7)]
    c = [(-1.0) ** i / math.factorial(2 * i) for i in range(7)]
    ps = jnp.full_like(z, s[-1])
    for v in s[-2::-1]:
        ps = ps * z + v
    pc = jnp.full_like(z, c[-1])
    for v in c[-2::-1]:
        pc = pc * z + v
    sn = ps * x
    return 1.0 - 2.0 * sn * sn, 2.0 * sn * pc


def fold(v):
    tiles = [
        v[r : r + 8, c : c + 128] for r in range(0, v.shape[0], 8) for c in range(0, v.shape[1], 128)
    ]
    while len(tiles) > 1:
        tiles = [sum(tiles[i : i + 2]) for i in range(0, len(tiles), 2)]
    return tiles[0]


def kernel(
    f_in, b1_in, b2_in, p1_in, p2_in, h_in, m1_out, m2_out, a_out,
    f, b, ph, cs, h, raws, px, prod, raw, irecv, wrecv, part, zrecv, precv, prow,
    both, full, m1, m1recv, mask, g, yb, s, arr, ls, ss, rs,
):
    mode = lax.axis_index("mode")
    row = lax.axis_index("row")
    zl, yc = mode // 8, lax.rem(mode, 8)
    zh, x = row // 4, lax.rem(row, 4)

    def row_peer(k):
        return (mode, lax.rem(row + k, 8))

    def x_peer(k):
        return (mode, zh * 4 + lax.rem(x + k, 4))

    def yc_peer(k):
        return (zl * 8 + lax.rem(yc + k, 8), row)

    def z_peer(k):
        return (lax.rem(zl + k, 8) * 8 + yc, row)

    def z16_peer(k):
        z = lax.rem(zh * 8 + zl + k, 16)
        return (lax.rem(z, 8) * 8 + yc, (z // 8) * 4 + x)

    def y_peer(k):
        return (zl * 8 + lax.rem(yc + 2 * k, 8), row)

    def c_peer(k):
        return (mode + 1 - 2 * lax.rem(mode, 2), row)

    def xyc_peer(k):
        at = lax.rem(x * 8 + yc + k, 32)
        return (zl * 8 + lax.rem(at, 8), zh * 4 + at // 8)

    bar = pltpu.get_barrier_semaphore()

    def greet(last, peer):
        def body(k, _):
            pl.semaphore_signal(bar, inc=1, device_id=peer(k), device_id_type=MESH)
            return 0

        lax.fori_loop(1, last, body, 0)

    greet(8, row_peer)
    greet(16, z16_peer)
    greet(32, xyc_peer)

    loads = [
        pltpu.make_async_copy(src, dst, ls.at[i])
        for i, (src, dst) in enumerate(
            [(f_in, f), (b1_in, b.at[0]), (p1_in, ph.at[0]), (h_in, h), (b2_in, b.at[1]), (p2_in, ph.at[1])]
        )
    ]
    for c in loads:
        c.start()

    used = [0, 0]
    sent = []

    class Stage:
        def __init__(self, src, dst, peer, all_sent, all_came=None, came=1):
            self.src, self.dst, self.peer, self.all_came = src, dst, peer, all_came
            self.s, self.r = used
            used[0] += 1
            used[1] += came
            self.left = lambda: self.desc(0, 0, all_sent).wait_send()
            sent.append(self)

        def desc(self, k, slot=0, whole=None):
            return pltpu.make_async_remote_copy(
                src_ref=self.src(k) if whole is None else whole,
                dst_ref=self.dst(k) if whole is None else whole,
                send_sem=ss.at[self.s], recv_sem=rs.at[self.r + slot],
                device_id=self.peer(1), device_id_type=MESH,
            )

        def start(self, k, slot=0):
            pltpu.make_async_remote_copy(
                src_ref=self.src(k), dst_ref=self.dst(k), send_sem=ss.at[self.s],
                recv_sem=rs.at[self.r + slot], device_id=self.peer(k), device_id_type=MESH,
            ).start()

        def start_all(self, last, first=1):
            def body(k, _):
                self.start(k)
                return 0

            lax.fori_loop(first, last, body, 0)

        def wait(self, whole=None, slot=0):
            self.desc(0, slot, self.all_came if whole is None else whole).wait_recv()

    def sixteen(j):
        return pl.ds(pl.multiple_of(j * 16, 16), 16)

    def products(i, front, put, turned):
        back = b.at[i]

        def body(j, acc):
            rows = sixteen(j)
            fr, fi = front[0, rows, :].astype(F32), front[1, rows, :].astype(F32)
            br, bi = back[0, rows, :].astype(F32), back[1, rows, :].astype(F32)
            pr = br * fr + bi * fi
            pi = br * fi - bi * fr
            for q in range(8):
                cols = slice(q * 128, q * 128 + 128)
                put(j, q, jnp.stack([pr[:, cols], pi[:, cols]]).astype(BF16))
            c, sn = turned(rows)
            return acc[0] + fold(pr * c - pi * sn), acc[1] + fold(pr * sn + pi * c)

        zero = jnp.zeros((8, 128), F32)
        ir, ii = lax.fori_loop(0, 8, body, (zero, zero))
        irecv[i, 0, 0] = jnp.sum(ir, axis=0, keepdims=True)
        irecv[i, 0, 1] = jnp.sum(ii, axis=0, keepdims=True)

    def overlap(i):
        st = Stage(
            lambda k: irecv.at[i, 0], lambda k: irecv.at[i, k], row_peer,
            irecv.at[i, pl.ds(1, 7)], irecv.at[i, pl.ds(1, 7)],
        )
        st.start_all(8)
        return st

    def share_products(i):
        st = Stage(
            lambda k: prod.at[i, lax.rem(yc + k, 8)], lambda k: raw.at[i, k], yc_peer,
            raw.at[i, pl.ds(1, 7)], raw.at[i, pl.ds(1, 7)],
        )
        st.start_all(8)
        return st

    def share_weights(i):
        for q in range(2):
            wrecv[i, 0, q] = sum(irecv[i, k, q] for k in range(8))
        st = Stage(
            lambda k: wrecv.at[i, 0], lambda k: wrecv.at[i, k], yc_peer,
            wrecv.at[i, pl.ds(1, 7)], wrecv.at[i, pl.ds(1, 7)],
        )
        st.start_all(8)
        return st

    def reduced(i):
        weights = [
            [jnp.sum(wrecv[i, k, q], axis=1, keepdims=True) * (1.0 / GRID) for q in range(2)]
            for k in range(8)
        ]
        st = Stage(
            lambda k: part.at[i, k], lambda k: zrecv.at[i, k], z_peer,
            zrecv.at[i, pl.ds(1, 7)], zrecv.at[i, pl.ds(1, 7)],
        )

        def body(k, _):
            q = lax.rem(zl + k, 8)
            tr = jnp.zeros((16, 128), F32)
            ti = jnp.zeros((16, 128), F32)
            for m in range(8):
                pr, pi = raw[i, m, q, 0].astype(F32), raw[i, m, q, 1].astype(F32)
                wr, wi = weights[m]
                tr = tr + (wr * pr + wi * pi)
                ti = ti + (wr * pi - wi * pr)
            part[i, k, 0] = tr.astype(BF16)
            part[i, k, 1] = ti.astype(BF16)

            @pl.when(k < 8)
            def _():
                st.start(k)

            return 0

        lax.fori_loop(1, 9, body, 0)
        zrecv[i, 0] = part[i, 8]
        st.wait()
        return sum(zrecv[i, k].astype(F32) for k in range(8)).astype(BF16)

    def power_z(i, piece):
        v = piece.astype(F32)
        precv[i, 0] = jnp.sum(fold(v[0] * v[0] + v[1] * v[1]), axis=0, keepdims=True)
        st = Stage(
            lambda k: precv.at[i, 0], lambda k: precv.at[i, k], z16_peer,
            precv.at[i, pl.ds(1, 15)], precv.at[i, pl.ds(1, 15)],
        )
        st.start_all(16)
        return st

    def power_xy(i):
        prow[i, 0] = sum(precv[i, k] for k in range(16))
        st = Stage(
            lambda k: prow.at[i, 0], lambda k: prow.at[i, k], xyc_peer,
            prow.at[i, pl.ds(1, 31)], prow.at[i, pl.ds(1, 31)],
        )
        st.start_all(32)
        return st

    def power_floor(i):
        total = sum(prow[i, k] for k in range(32))
        mean = jnp.sum(total, axis=1, keepdims=True) * (1.0 / (GRID * GRID))
        return 0.25 * mean + 1e-6

    def masked(piece, floor):
        v = piece.astype(F32)
        scale = lax.rsqrt(v[0] * v[0] + v[1] * v[1] + floor)
        return (v[0] * scale).astype(BF16), (-v[1] * scale).astype(BF16)

    for c in loads[:3]:
        c.wait()

    def put_first(j, q, pair):
        px[q // 2, j // 4, lax.rem(j, 4) * 2 + q % 2] = pair

    products(0, f, put_first, lambda rows: cos_sin(ph[0, rows, :]))
    pl.semaphore_wait(bar, 7 + 15 + 31)
    over = overlap(0)
    turn = Stage(
        lambda k: px.at[lax.rem(x + k, 4)], lambda k: prod.at[0, pl.ds(2 * x, 2)], x_peer,
        prod.at[0, pl.ds(0, 6)], prod.at[0, pl.ds(0, 6)],
    )
    turn.start_all(4)

    def block(r, half):
        return pl.ds(pl.multiple_of(lax.rem(r, 4) * 256 + half * 128, 128), 128)

    moves = []
    parts = ((0, 0, 128), (1, 0, 64), (1, 64, 64))
    for half, top, size in parts:
        some = pl.ds(top, size)
        st = Stage(
            lambda k, half=half, some=some: f.at[:, some, block(row + k, half)],
            lambda k, half=half, some=some: raws.at[half, row, :, some, :], row_peer,
            raws.at[half, pl.ds(0, 7), :, some, :], raws.at[half, pl.ds(0, 7), :, some, :],
        )
        moves.append(st)

    def far(k):
        return (lax.rem(row + k, 8) // 4) != zh

    def move(part, want_far):
        def body(k, _):
            @pl.when(far(k) if want_far else jnp.logical_not(far(k)))
            def _():
                moves[part].start(k)

            return 0

        lax.fori_loop(1, 8, body, 0)

    move(0, True)
    own = [
        pltpu.make_async_copy(f.at[:, :, block(row, half)], raws.at[half, row], ls.at[9 + half])
        for half in range(2)
    ]
    for c in own:
        c.start()
    prod[0, pl.ds(2 * x, 2)] = px[x]
    turn.wait()
    share = share_products(0)
    for p in range(3):
        move(p, False)
    over.wait()
    weight = share_weights(0)
    raw[0, 0] = prod[0, yc]
    share.wait()
    weight.wait()
    piece = reduced(0)
    both[yc, 2 * zl + zh] = piece
    gather_z = Stage(
        lambda k: both.at[yc, 2 * zl + zh], lambda k: both.at[yc, 2 * zl + zh], z16_peer,
        both.at[yc, pl.ds(0, 15)], both.at[yc, pl.ds(0, 15)],
    )
    gather_z.start_all(16)
    pz = power_z(0, piece)
    gather_z.wait()
    move(1, True)
    move(2, True)
    gather_y = Stage(
        lambda k: both.at[yc], lambda k: both.at[yc], y_peer, both.at[pl.ds(0, 3)], None, 3
    )
    for o in range(1, 4):
        gather_y.start(o, o - 1)
    gather_c = Stage(
        lambda k: both.at[lax.rem(yc + 2 * k, 8)], lambda k: both.at[lax.rem(yc + 2 * k, 8)], c_peer,
        both.at[pl.ds(0, 4)], both.at[pl.ds(0, 4)],
    )
    gather_c.start(4)
    pz.wait()
    pxy = power_xy(0)
    for o in range(1, 4):
        gather_y.wait(both.at[0], o - 1)
        gather_c.start(4 - o)
    pxy.wait()
    floor = power_floor(0)
    gather_c.wait()

    def make_mask(n, _):
        for q in range(8):
            for z in range(2):
                mr, mi = masked(both[n, 2 * q + z], floor)
                both[n, 2 * q + z, 0] = mr
                both[n, 2 * q + z, 1] = mi
            m1[n, q] = both[n, 2 * q + zh]
        return 0

    early = [gather_z, gather_y, gather_c]
    for st in early:
        st.left()
    lax.fori_loop(0, 8, make_mask, 0)
    back1 = Stage(
        lambda k: m1.at[pl.ds(2 * lax.rem(x + k, 4), 2)], lambda k: m1recv.at[x], x_peer,
        m1recv.at[pl.ds(0, 3)], m1recv.at[pl.ds(0, 3)],
    )
    back1.start_all(4)
    m1recv[x] = m1[pl.ds(2 * x, 2)]
    for c in own:
        c.wait()
    for c in loads[3:]:
        c.wait()

    def turn_phase(j, _):
        c, sn = cos_sin(ph[1, sixteen(j), :])
        cs[0, sixteen(j), :] = c
        cs[1, sixteen(j), :] = sn
        return 0

    lax.fori_loop(0, 8, turn_phase, 0)

    to_rows = []
    for half in range(2):
        for p in (0,) if half == 0 else (1, 2):
            moves[p].wait()

        def apply(j, _, half=half):
            z, n = j // 8, lax.rem(j, 8)
            for u in range(4):
                v = both[n, (2 * u + half) * 2 + z].astype(F32)
                at = lax.rem(n, 2) * 64 + u * 16
                rows = pl.ds(pl.multiple_of(at, 16), 16)
                fr = raws[half, z * 4 + n // 2, 0, rows, :].astype(F32)
                fi = raws[half, z * 4 + n // 2, 1, rows, :].astype(F32)
                mr, mi = v[0], v[1]
                rows = pl.ds(pl.multiple_of(j * 64 + u * 16, 16), 16)
                g[half, rows, 0:128] = (fr * mr - fi * mi).astype(BF16)
                g[half, rows, 128:256] = (fr * mi + fi * mr).astype(BF16)
            return 0

        lax.fori_loop(0, 16, apply, 0)
        st = Stage(
            lambda k, half=half: yb.at[half, lax.rem(x + k, 4)],
            lambda k, half=half: s.at[:, :, pl.ds(pl.multiple_of(x * 256 + half * 128, 128), 128)],
            x_peer, yb.at[half, pl.ds(0, 3)], yb.at[half, pl.ds(0, 3)],
        )
        to_rows.append(st)
        for n in range(2):
            rows = pl.ds(pl.multiple_of(zh * 512 + n * 256, 256), 256)
            a = jnp.dot(h[0, rows, :], g[half], preferred_element_type=F32)
            c = jnp.dot(h[1, rows, :], g[half], preferred_element_type=F32)
            yr = (a[:, :128] - c[:, 128:]).astype(BF16)
            yi = (a[:, 128:] + c[:, :128]).astype(BF16)
            for e in range(2):
                to = 2 * n + e
                yb[half, to, 0] = yr[e * ROWS : e * ROWS + ROWS]
                yb[half, to, 1] = yi[e * ROWS : e * ROWS + ROWS]

                @pl.when(to != x)
                def _(to=to, st=st):
                    st.start(lax.rem(to - x + 4, 4))

        s[:, :, pl.ds(pl.multiple_of(x * 256 + half * 128, 128), 128)] = yb[half, x]

    for half in range(2):
        to_rows[half].wait()

    def columns(n, _):
        cols = pl.ds(pl.multiple_of(n * 256, 256), 256)
        field = s[...].reshape(2 * ROWS, GRID)
        a = jnp.dot(field, h[0, :, cols], preferred_element_type=F32)
        c = jnp.dot(field, h[1, :, cols], preferred_element_type=F32)
        arr[0, :, cols] = (a[:ROWS] - c[ROWS:]).astype(BF16)
        arr[1, :, cols] = (c[:ROWS] + a[ROWS:]).astype(BF16)
        return 0

    lax.fori_loop(0, 4, columns, 0)
    outs = [pltpu.make_async_copy(arr, a_out, ls.at[6])]
    outs[0].start()

    def put_second(j, q, pair):
        prod[1, j, q] = pair

    products(1, arr, put_second, lambda rows: (cs[0, rows, :], cs[1, rows, :]))
    over = overlap(1)
    share = share_products(1)
    over.wait()
    weight = share_weights(1)
    raw[1, 0] = prod[1, yc]
    share.wait()
    weight.wait()
    piece = reduced(1)
    full[yc, zl] = piece
    gather_z = Stage(
        lambda k: full.at[yc, zl], lambda k: full.at[yc, zl], z_peer, full.at[yc, pl.ds(0, 7)], None, 8
    )

    def spread(k, _):
        gather_z.start(k, zl)
        return 0

    lax.fori_loop(1, 8, spread, 0)
    pz = power_z(1, piece)

    gather_y2 = [
        Stage(lambda q: full.at[yc, q], lambda q: full.at[yc, q], lambda k, o=o: y_peer(o), full.at[yc], full.at[0])
        for o in range(1, 4)
    ]

    def onward(q):
        for st in gather_y2:
            st.start(q)

    onward(zl)

    def forward(d, _):
        for q in (zl - d, zl + d):

            @pl.when((q >= 0) & (q < 8))
            def _():
                gather_z.wait(full.at[yc, q], q)
                onward(q)

        return 0

    lax.fori_loop(1, 8, forward, 0)
    gather_c = Stage(
        lambda k: full.at[lax.rem(yc + 2 * k, 8)], lambda k: full.at[lax.rem(yc + 2 * k, 8)], c_peer,
        full.at[pl.ds(0, 4)], full.at[pl.ds(0, 4)],
    )
    gather_c.start(4)
    pz.wait()
    pxy = power_xy(1)
    for o in range(1, 4):
        gather_y2[o - 1].wait()
        gather_c.start(4 - o)

    back1.wait()

    def lay(j, _):
        for q in range(8):
            v = m1recv[q // 2, j // 4, lax.rem(j, 4) * 2 + q % 2]
            mask[0, 0, sixteen(j), q * 128 : q * 128 + 128] = v[0]
            mask[0, 1, sixteen(j), q * 128 : q * 128 + 128] = v[1]
        return 0

    lax.fori_loop(0, 8, lay, 0)
    outs.append(pltpu.make_async_copy(mask.at[0], m1_out, ls.at[7]))
    outs[1].start()
    pxy.wait()
    floor2 = power_floor(1)
    gather_c.wait()

    def finish(j, _):
        for q in range(8):
            mr, mi = masked(full[j, q], floor2)
            mask[1, 0, sixteen(j), q * 128 : q * 128 + 128] = mr
            mask[1, 1, sixteen(j), q * 128 : q * 128 + 128] = mi
        return 0

    lax.fori_loop(0, 8, finish, 0)
    outs.append(pltpu.make_async_copy(mask.at[1], m2_out, ls.at[8]))
    outs[2].start()
    for st in sent:
        if st not in early:
            st.left()
    for c in outs:
        c.wait()


def on_device(forward, backward_first, backward_second, phase_first, phase_second):
    hbm = pl.BlockSpec(memory_space=pl.ANY)
    block = (2, ROWS, GRID)
    tile = (2, 16, 128)
    m1, m2, arrived = pl.pallas_call(
        kernel,
        out_shape=[jax.ShapeDtypeStruct(block, BF16)] * 3,
        in_specs=[hbm] * 6,
        out_specs=[hbm] * 3,
        scratch_shapes=[
            pltpu.VMEM(block, BF16),
            pltpu.VMEM((2, *block), BF16),
            pltpu.VMEM((2, ROWS, GRID), F32),
            pltpu.VMEM((2, ROWS, GRID), F32),
            pltpu.VMEM((2, GRID, GRID), BF16),
            pltpu.VMEM((2, 8, 2, ROWS, 128), BF16),
            pltpu.VMEM((4, 2, 8, *tile), BF16),
            pltpu.VMEM((2, 8, 8, *tile), BF16),
            pltpu.VMEM((2, 8, 8, *tile), BF16),
            pltpu.VMEM((2, 8, 2, 1, 128), F32),
            pltpu.VMEM((2, 8, 2, 1, 128), F32),
            pltpu.VMEM((2, 9, *tile), BF16),
            pltpu.VMEM((2, 8, *tile), BF16),
            pltpu.VMEM((2, 16, 1, 128), F32),
            pltpu.VMEM((2, 32, 1, 128), F32),
            pltpu.VMEM((8, 16, *tile), BF16),
            pltpu.VMEM((8, 8, *tile), BF16),
            pltpu.VMEM((8, 8, *tile), BF16),
            pltpu.VMEM((4, 2, 8, *tile), BF16),
            pltpu.VMEM((2, *block), BF16),
            pltpu.VMEM((2, GRID, 256), BF16),
            pltpu.VMEM((2, 4, 2, ROWS, 128), BF16),
            pltpu.VMEM(block, BF16),
            pltpu.VMEM(block, BF16),
            pltpu.SemaphoreType.DMA((11,)),
            pltpu.SemaphoreType.DMA((32,)),
            pltpu.SemaphoreType.DMA((40,)),
        ],
        compiler_params=pltpu.CompilerParams(
            collective_id=0, has_side_effects=True, vmem_limit_bytes=52 * 2**20
        ),
    )(
        forward[0], backward_first[0], backward_second[0], phase_first, phase_second,
        jnp.asarray(propagator()),
    )
    return m1, m2, arrived[None]


def solution(mesh):
    in_specs = (
        P("mode", None, "row", None),
        P("mode", None, "row", None),
        P("mode", None, "row", None),
        P("row", None),
        P("row", None),
    )
    out_specs = (P(None, "row", None), P(None, "row", None), P("mode", None, "row", None))
    return jax.shard_map(
        on_device, mesh=mesh, in_specs=in_specs, out_specs=out_specs, check_vma=False
    )
```

```python
import functools
import math

import jax
import jax.numpy as jnp
import ml_dtypes
import numpy as np
from jax import lax
from jax.experimental import pallas as pl
from jax.experimental.pallas import tpu as pltpu
from jax.sharding import PartitionSpec as P

GRID = 1024
ROWS = 128
MESH = pl.DeviceIdType.MESH
F32 = jnp.float32
BF16 = jnp.bfloat16


@functools.cache
def propagator():
    u = np.arange(GRID)
    turns = u[:, None] * u[None, :] % GRID
    angles = np.minimum(turns, GRID - turns) * (2.0 * math.pi / GRID)
    sign = np.where(turns <= GRID // 2, 1.0, -1.0)
    cosine = np.cos(angles).astype(ml_dtypes.bfloat16).astype(np.float64)
    sine = (sign * np.sin(angles)).astype(ml_dtypes.bfloat16).astype(np.float64)
    f = (u + GRID // 2) % GRID - GRID // 2
    phases = (f * f % (2 * GRID)) * (math.pi / GRID)
    chirp = np.cos(phases) - 1j * np.sin(phases)
    h = ((cosine - 1j * sine) * chirp) @ (cosine + 1j * sine) / GRID
    return np.stack([h.real, h.imag]).astype(ml_dtypes.bfloat16)


def cos_sin(phase):
    x = phase * 0.5
    z = x * x
    s = [(-1.0) ** i / math.factorial(2 * i + 1) for i in range(7)]
    c = [(-1.0) ** i / math.factorial(2 * i) for i in range(7)]
    ps = jnp.full_like(z, s[-1])
    for v in s[-2::-1]:
        ps = ps * z + v
    pc = jnp.full_like(z, c[-1])
    for v in c[-2::-1]:
        pc = pc * z + v
    sn = ps * x
    return 1.0 - 2.0 * sn * sn, 2.0 * sn * pc


def fold(v):
    tiles = [
        v[r : r + 8, c : c + 128] for r in range(0, v.shape[0], 8) for c in range(0, v.shape[1], 128)
    ]
    while len(tiles) > 1:
        tiles = [sum(tiles[i : i + 2]) for i in range(0, len(tiles), 2)]
    return tiles[0]


def kernel(
    f_in, b1_in, b2_in, p1_in, p2_in, h_in, m1_out, m2_out, a_out,
    f, b, ph, cs, h, hk, acc, raws, px, prod, raw, irecv, wrecv, part, zrecv, precv, prow,
    both, full, m1, m1recv, mask, g, yb, s, arr, ls, ss, rs,
):
    mode = lax.axis_index("mode")
    row = lax.axis_index("row")
    zl, yc = mode // 8, lax.rem(mode, 8)
    zh, x = row // 4, lax.rem(row, 4)

    def row_peer(k):
        return (mode, lax.rem(row + k, 8))

    def x_peer(k):
        return (mode, zh * 4 + lax.rem(x + k, 4))

    def yc_peer(k):
        return (zl * 8 + lax.rem(yc + k, 8), row)

    def z_peer(k):
        return (lax.rem(zl + k, 8) * 8 + yc, row)

    def z16_peer(k):
        z = lax.rem(zh * 8 + zl + k, 16)
        return (lax.rem(z, 8) * 8 + yc, (z // 8) * 4 + x)

    def y_peer(k):
        return (zl * 8 + lax.rem(yc + 2 * k, 8), row)

    def c_peer(k):
        return (mode + 1 - 2 * lax.rem(mode, 2), row)

    def xyc_peer(k):
        at = lax.rem(x * 8 + yc + k, 32)
        return (zl * 8 + lax.rem(at, 8), zh * 4 + at // 8)

    bar = pltpu.get_barrier_semaphore()

    def greet(last, peer):
        def body(k, _):
            pl.semaphore_signal(bar, inc=1, device_id=peer(k), device_id_type=MESH)
            return 0

        lax.fori_loop(1, last, body, 0)

    greet(8, row_peer)
    greet(16, z16_peer)
    greet(32, xyc_peer)

    loads = [
        pltpu.make_async_copy(src, dst, ls.at[i])
        for i, (src, dst) in enumerate(
            [(f_in, f), (b1_in, b.at[0]), (p1_in, ph.at[0]), (h_in, h), (b2_in, b.at[1]), (p2_in, ph.at[1])]
        )
    ]
    loads += [
        pltpu.make_async_copy(
            h_in.at[:, pl.ds(v * 256 + half * 128, 128), :],
            hk.at[:, half, pl.ds(v * 128, 128), :], ls.at[11 + half * 4 + v],
        )
        for half in range(2)
        for v in range(4)
    ]
    for c in loads:
        c.start()

    used = [0, 0]
    sent = []

    class Stage:
        def __init__(self, src, dst, peer, all_sent, all_came=None, came=1):
            self.src, self.dst, self.peer, self.all_came = src, dst, peer, all_came
            self.s, self.r = used
            used[0] += 1
            used[1] += came
            self.left = lambda: self.desc(0, 0, all_sent).wait_send()
            sent.append(self)

        def desc(self, k, slot=0, whole=None):
            return pltpu.make_async_remote_copy(
                src_ref=self.src(k) if whole is None else whole,
                dst_ref=self.dst(k) if whole is None else whole,
                send_sem=ss.at[self.s], recv_sem=rs.at[self.r + slot],
                device_id=self.peer(1), device_id_type=MESH,
            )

        def start(self, k, slot=0):
            pltpu.make_async_remote_copy(
                src_ref=self.src(k), dst_ref=self.dst(k), send_sem=ss.at[self.s],
                recv_sem=rs.at[self.r + slot], device_id=self.peer(k), device_id_type=MESH,
            ).start()

        def start_all(self, last, first=1):
            def body(k, _):
                self.start(k)
                return 0

            lax.fori_loop(first, last, body, 0)

        def wait(self, whole=None, slot=0):
            self.desc(0, slot, self.all_came if whole is None else whole).wait_recv()

    def sixteen(j):
        return pl.ds(pl.multiple_of(j * 16, 16), 16)

    def products(i, front, put, turned):
        back = b.at[i]

        def body(j, acc):
            rows = sixteen(j)
            fr, fi = front[0, rows, :].astype(F32), front[1, rows, :].astype(F32)
            br, bi = back[0, rows, :].astype(F32), back[1, rows, :].astype(F32)
            pr = br * fr + bi * fi
            pi = br * fi - bi * fr
            for q in range(8):
                cols = slice(q * 128, q * 128 + 128)
                put(j, q, jnp.stack([pr[:, cols], pi[:, cols]]).astype(BF16))
            c, sn = turned(rows)
            return acc[0] + fold(pr * c - pi * sn), acc[1] + fold(pr * sn + pi * c)

        zero = jnp.zeros((8, 128), F32)
        ir, ii = lax.fori_loop(0, 8, body, (zero, zero))
        irecv[i, 0, 0] = jnp.sum(ir, axis=0, keepdims=True)
        irecv[i, 0, 1] = jnp.sum(ii, axis=0, keepdims=True)

    def overlap(i):
        st = Stage(
            lambda k: irecv.at[i, 0], lambda k: irecv.at[i, k], row_peer,
            irecv.at[i, pl.ds(1, 7)], irecv.at[i, pl.ds(1, 7)],
        )
        st.start_all(8)
        return st

    def share_products(i):
        st = Stage(
            lambda k: prod.at[i, lax.rem(yc + k, 8)], lambda k: raw.at[i, k], yc_peer,
            raw.at[i, pl.ds(1, 7)], raw.at[i, pl.ds(1, 7)],
        )
        st.start_all(8)
        return st

    def share_weights(i):
        for q in range(2):
            wrecv[i, 0, q] = sum(irecv[i, k, q] for k in range(8))
        st = Stage(
            lambda k: wrecv.at[i, 0], lambda k: wrecv.at[i, k], yc_peer,
            wrecv.at[i, pl.ds(1, 7)], wrecv.at[i, pl.ds(1, 7)],
        )
        st.start_all(8)
        return st

    def reduced(i):
        weights = [
            [jnp.sum(wrecv[i, k, q], axis=1, keepdims=True) * (1.0 / GRID) for q in range(2)]
            for k in range(8)
        ]
        st = Stage(
            lambda k: part.at[i, k], lambda k: zrecv.at[i, k], z_peer,
            zrecv.at[i, pl.ds(1, 7)], zrecv.at[i, pl.ds(1, 7)],
        )

        def body(k, _):
            q = lax.rem(zl + k, 8)
            tr = jnp.zeros((16, 128), F32)
            ti = jnp.zeros((16, 128), F32)
            for m in range(8):
                pr, pi = raw[i, m, q, 0].astype(F32), raw[i, m, q, 1].astype(F32)
                wr, wi = weights[m]
                tr = tr + (wr * pr + wi * pi)
                ti = ti + (wr * pi - wi * pr)
            part[i, k, 0] = tr.astype(BF16)
            part[i, k, 1] = ti.astype(BF16)

            @pl.when(k < 8)
            def _():
                st.start(k)

            return 0

        lax.fori_loop(1, 9, body, 0)
        zrecv[i, 0] = part[i, 8]
        st.wait()
        return sum(zrecv[i, k].astype(F32) for k in range(8)).astype(BF16)

    def power_z(i, piece):
        v = piece.astype(F32)
        precv[i, 0] = jnp.sum(fold(v[0] * v[0] + v[1] * v[1]), axis=0, keepdims=True)
        st = Stage(
            lambda k: precv.at[i, 0], lambda k: precv.at[i, k], z16_peer,
            precv.at[i, pl.ds(1, 15)], precv.at[i, pl.ds(1, 15)],
        )
        st.start_all(16)
        return st

    def power_xy(i):
        prow[i, 0] = sum(precv[i, k] for k in range(16))
        st = Stage(
            lambda k: prow.at[i, 0], lambda k: prow.at[i, k], xyc_peer,
            prow.at[i, pl.ds(1, 31)], prow.at[i, pl.ds(1, 31)],
        )
        st.start_all(32)
        return st

    def power_floor(i):
        total = sum(prow[i, k] for k in range(32))
        mean = jnp.sum(total, axis=1, keepdims=True) * (1.0 / (GRID * GRID))
        return 0.25 * mean + 1e-6

    def masked(piece, floor):
        v = piece.astype(F32)
        scale = lax.rsqrt(v[0] * v[0] + v[1] * v[1] + floor)
        return (v[0] * scale).astype(BF16), (-v[1] * scale).astype(BF16)

    for c in loads[:3]:
        c.wait()

    def put_first(j, q, pair):
        px[q // 2, j // 4, lax.rem(j, 4) * 2 + q % 2] = pair

    products(0, f, put_first, lambda rows: cos_sin(ph[0, rows, :]))
    pl.semaphore_wait(bar, 7 + 15 + 31)
    over = overlap(0)
    turn = Stage(
        lambda k: px.at[lax.rem(x + k, 4)], lambda k: prod.at[0, pl.ds(2 * x, 2)], x_peer,
        prod.at[0, pl.ds(0, 6)], prod.at[0, pl.ds(0, 6)],
    )
    turn.start_all(4)

    def block(r, half):
        return pl.ds(pl.multiple_of(lax.rem(r, 4) * 256 + half * 128, 128), 128)

    moves = []
    parts = ((0, 0, 128), (1, 0, 64), (1, 64, 64))
    for half, top, size in parts:
        some = pl.ds(top, size)
        st = Stage(
            lambda k, half=half, some=some: f.at[:, some, block(row + k, half)],
            lambda k, half=half, some=some: raws.at[half, row, :, some, :], row_peer,
            raws.at[half, pl.ds(0, 7), :, some, :], raws.at[half, pl.ds(0, 7), :, some, :],
        )
        moves.append(st)

    def far(k):
        return (lax.rem(row + k, 8) // 4) != zh

    def move(part, want_far):
        def body(k, _):
            @pl.when(far(k) if want_far else jnp.logical_not(far(k)))
            def _():
                moves[part].start(k)

            return 0

        lax.fori_loop(1, 8, body, 0)

    move(0, True)
    own = [
        pltpu.make_async_copy(f.at[:, :, block(row, half)], raws.at[half, row], ls.at[9 + half])
        for half in range(2)
    ]
    for c in own:
        c.start()
    prod[0, pl.ds(2 * x, 2)] = px[x]
    turn.wait()
    share = share_products(0)
    for p in range(3):
        move(p, False)
    over.wait()
    weight = share_weights(0)
    raw[0, 0] = prod[0, yc]
    share.wait()
    weight.wait()
    piece = reduced(0)
    both[yc, 2 * zl + zh] = piece
    gather_z = Stage(
        lambda k: both.at[yc, 2 * zl + zh], lambda k: both.at[yc, 2 * zl + zh], z16_peer,
        both.at[yc, pl.ds(0, 15)], both.at[yc, pl.ds(0, 15)],
    )
    gather_z.start_all(16)
    pz = power_z(0, piece)
    gather_z.wait()
    move(1, True)
    move(2, True)
    gather_y = Stage(
        lambda k: both.at[yc], lambda k: both.at[yc], y_peer, both.at[pl.ds(0, 3)], None, 3
    )
    for o in range(1, 4):
        gather_y.start(o, o - 1)
    gather_c = Stage(
        lambda k: both.at[lax.rem(yc + 2 * k, 8)], lambda k: both.at[lax.rem(yc + 2 * k, 8)], c_peer,
        both.at[pl.ds(0, 4)], both.at[pl.ds(0, 4)],
    )
    gather_c.start(4)
    pz.wait()
    pxy = power_xy(0)
    for o in range(1, 4):
        gather_y.wait(both.at[0], o - 1)
        gather_c.start(4 - o)
    pxy.wait()
    floor = power_floor(0)
    gather_c.wait()

    def make_mask(n, _):
        for q in range(8):
            for z in range(2):
                mr, mi = masked(both[n, 2 * q + z], floor)
                both[n, 2 * q + z, 0] = mr
                both[n, 2 * q + z, 1] = mi
            m1[n, q] = both[n, 2 * q + zh]
        return 0

    early = [gather_z, gather_y, gather_c]
    for st in early:
        st.left()
    lax.fori_loop(0, 8, make_mask, 0)
    back1 = Stage(
        lambda k: m1.at[pl.ds(2 * lax.rem(x + k, 4), 2)], lambda k: m1recv.at[x], x_peer,
        m1recv.at[pl.ds(0, 3)], m1recv.at[pl.ds(0, 3)],
    )
    back1.start_all(4)
    m1recv[x] = m1[pl.ds(2 * x, 2)]
    for c in own:
        c.wait()
    for c in loads[3:]:
        c.wait()

    def turn_phase(j, _):
        c, sn = cos_sin(ph[1, sixteen(j), :])
        cs[0, sixteen(j), :] = c
        cs[1, sixteen(j), :] = sn
        return 0

    lax.fori_loop(0, 8, turn_phase, 0)

    def columns(half, n, _):
        cols = pl.ds(pl.multiple_of(n * 256, 256), 256)
        field = s[half].reshape(2 * ROWS, GRID // 2)
        a = jnp.dot(field, hk[0, half, :, cols], preferred_element_type=F32)
        c = jnp.dot(field, hk[1, half, :, cols], preferred_element_type=F32)
        re, im = a[:ROWS] - c[ROWS:], c[:ROWS] + a[ROWS:]
        if half == 0:
            acc[0, :, cols] = re
            acc[1, :, cols] = im
        else:
            arr[0, :, cols] = (acc[0, :, cols] + re).astype(BF16)
            arr[1, :, cols] = (acc[1, :, cols] + im).astype(BF16)
        return 0

    for half in range(2):
        for p in (0,) if half == 0 else (1, 2):
            moves[p].wait()

        def apply(j, _, half=half):
            z, n = j // 8, lax.rem(j, 8)
            for u in range(4):
                v = both[n, (2 * u + half) * 2 + z].astype(F32)
                at = lax.rem(n, 2) * 64 + u * 16
                rows = pl.ds(pl.multiple_of(at, 16), 16)
                fr = raws[half, z * 4 + n // 2, 0, rows, :].astype(F32)
                fi = raws[half, z * 4 + n // 2, 1, rows, :].astype(F32)
                mr, mi = v[0], v[1]
                rows = pl.ds(pl.multiple_of(j * 64 + u * 16, 16), 16)
                g[half, rows, 0:128] = (fr * mr - fi * mi).astype(BF16)
                g[half, rows, 128:256] = (fr * mi + fi * mr).astype(BF16)
            return 0

        lax.fori_loop(0, 16, apply, 0)
        st = Stage(
            lambda k, half=half: yb.at[half, lax.rem(x + k, 4)],
            lambda k, half=half: s.at[half, :, :, pl.ds(pl.multiple_of(x * 128, 128), 128)],
            x_peer, yb.at[half, pl.ds(0, 3)], yb.at[half, pl.ds(0, 3)],
        )
        for n in range(2):
            rows = pl.ds(pl.multiple_of(zh * 512 + n * 256, 256), 256)
            a = jnp.dot(h[0, rows, :], g[half], preferred_element_type=F32)
            c = jnp.dot(h[1, rows, :], g[half], preferred_element_type=F32)
            yr = (a[:, :128] - c[:, 128:]).astype(BF16)
            yi = (a[:, 128:] + c[:, :128]).astype(BF16)
            for e in range(2):
                to = 2 * n + e
                yb[half, to, 0] = yr[e * ROWS : e * ROWS + ROWS]
                yb[half, to, 1] = yi[e * ROWS : e * ROWS + ROWS]

                @pl.when(to != x)
                def _(to=to, st=st):
                    st.start(lax.rem(to - x + 4, 4))

        s[half, :, :, pl.ds(pl.multiple_of(x * 128, 128), 128)] = yb[half, x]
        st.wait()
        lax.fori_loop(0, 4, functools.partial(columns, half), 0)

    outs = [pltpu.make_async_copy(arr, a_out, ls.at[6])]
    outs[0].start()

    def put_second(j, q, pair):
        prod[1, j, q] = pair

    products(1, arr, put_second, lambda rows: (cs[0, rows, :], cs[1, rows, :]))
    over = overlap(1)
    share = share_products(1)
    over.wait()
    weight = share_weights(1)
    raw[1, 0] = prod[1, yc]
    share.wait()
    weight.wait()
    piece = reduced(1)
    full[yc, zl] = piece
    gather_z = Stage(
        lambda k: full.at[yc, zl], lambda k: full.at[yc, zl], z_peer, full.at[yc, pl.ds(0, 7)], None, 8
    )

    def spread(k, _):
        gather_z.start(k, zl)
        return 0

    pz = power_z(1, piece)
    lax.fori_loop(1, 8, spread, 0)

    gather_y2 = [
        Stage(lambda q: full.at[yc, q], lambda q: full.at[yc, q], lambda k, o=o: y_peer(o), full.at[yc], full.at[0])
        for o in range(1, 4)
    ]

    def onward(q):
        for st in gather_y2:
            st.start(q)

    onward(zl)

    def forward(d, _):
        for q in (zl - d, zl + d):

            @pl.when((q >= 0) & (q < 8))
            def _():
                gather_z.wait(full.at[yc, q], q)
                onward(q)

        return 0

    lax.fori_loop(1, 8, forward, 0)
    gather_c = Stage(
        lambda k: full.at[lax.rem(yc + 2 * k, 8)], lambda k: full.at[lax.rem(yc + 2 * k, 8)], c_peer,
        full.at[pl.ds(0, 4)], full.at[pl.ds(0, 4)],
    )
    gather_c.start(4)
    pz.wait()
    pxy = power_xy(1)
    for o in range(1, 4):
        gather_y2[o - 1].wait()
        gather_c.start(4 - o)

    back1.wait()

    def lay(j, _):
        for q in range(8):
            v = m1recv[q // 2, j // 4, lax.rem(j, 4) * 2 + q % 2]
            mask[0, 0, sixteen(j), q * 128 : q * 128 + 128] = v[0]
            mask[0, 1, sixteen(j), q * 128 : q * 128 + 128] = v[1]
        return 0

    lax.fori_loop(0, 8, lay, 0)
    outs.append(pltpu.make_async_copy(mask.at[0], m1_out, ls.at[7]))
    outs[1].start()
    pxy.wait()
    floor2 = power_floor(1)
    gather_c.wait()

    def finish(j, _):
        for q in range(8):
            mr, mi = masked(full[j, q], floor2)
            mask[1, 0, sixteen(j), q * 128 : q * 128 + 128] = mr
            mask[1, 1, sixteen(j), q * 128 : q * 128 + 128] = mi
        return 0

    lax.fori_loop(0, 8, finish, 0)
    outs.append(pltpu.make_async_copy(mask.at[1], m2_out, ls.at[8]))
    outs[2].start()
    for st in sent:
        if st not in early:
            st.left()
    for c in outs:
        c.wait()


def write_out(*refs):
    sems = refs[6]
    copies = []
    for src, dst in zip(refs[:3], refs[3:6]):
        for i in range(4):
            rows = pl.ds(i * 32, 32)
            copies.append(
                pltpu.make_async_copy(src.at[:, rows], dst.at[:, rows], sems.at[len(copies)])
            )
            copies[-1].start()
    for c in copies:
        c.wait()


def on_device(forward, backward_first, backward_second, phase_first, phase_second):
    hbm = pl.BlockSpec(memory_space=pl.ANY)
    block = (2, ROWS, GRID)
    tile = (2, 16, 128)
    m1, m2, arrived = pl.pallas_call(
        kernel,
        out_shape=[jax.ShapeDtypeStruct(block, BF16)] * 3,
        in_specs=[hbm] * 6,
        out_specs=[hbm] * 3,
        scratch_shapes=[
            pltpu.VMEM(block, BF16),
            pltpu.VMEM((2, *block), BF16),
            pltpu.VMEM((2, ROWS, GRID), F32),
            pltpu.VMEM((2, ROWS, GRID), F32),
            pltpu.VMEM((2, GRID, GRID), BF16),
            pltpu.VMEM((2, 2, GRID // 2, GRID), BF16),
            pltpu.VMEM(block, F32),
            pltpu.VMEM((2, 8, 2, ROWS, 128), BF16),
            pltpu.VMEM((4, 2, 8, *tile), BF16),
            pltpu.VMEM((2, 8, 8, *tile), BF16),
            pltpu.VMEM((2, 8, 8, *tile), BF16),
            pltpu.VMEM((2, 8, 2, 1, 128), F32),
            pltpu.VMEM((2, 8, 2, 1, 128), F32),
            pltpu.VMEM((2, 9, *tile), BF16),
            pltpu.VMEM((2, 8, *tile), BF16),
            pltpu.VMEM((2, 16, 1, 128), F32),
            pltpu.VMEM((2, 32, 1, 128), F32),
            pltpu.VMEM((8, 16, *tile), BF16),
            pltpu.VMEM((8, 8, *tile), BF16),
            pltpu.VMEM((8, 8, *tile), BF16),
            pltpu.VMEM((4, 2, 8, *tile), BF16),
            pltpu.VMEM((2, *block), BF16),
            pltpu.VMEM((2, GRID, 256), BF16),
            pltpu.VMEM((2, 4, 2, ROWS, 128), BF16),
            pltpu.VMEM((2, 2, ROWS, GRID // 2), BF16),
            pltpu.VMEM(block, BF16),
            pltpu.SemaphoreType.DMA((19,)),
            pltpu.SemaphoreType.DMA((32,)),
            pltpu.SemaphoreType.DMA((40,)),
        ],
        compiler_params=pltpu.CompilerParams(
            collective_id=0, has_side_effects=True, vmem_limit_bytes=52 * 2**20
        ),
    )(
        forward[0], backward_first[0], backward_second[0], phase_first, phase_second,
        jnp.asarray(propagator()),
    )
    m1, m2, arrived = pl.pallas_call(
        write_out,
        out_shape=[jax.ShapeDtypeStruct(block, BF16)] * 3,
        in_specs=[hbm] * 3,
        out_specs=[hbm] * 3,
        scratch_shapes=[pltpu.SemaphoreType.DMA((12,))],
        compiler_params=pltpu.CompilerParams(vmem_limit_bytes=2**20),
    )(m1, m2, arrived)
    return m1, m2, arrived[None]


def solution(mesh):
    in_specs = (
        P("mode", None, "row", None),
        P("mode", None, "row", None),
        P("mode", None, "row", None),
        P("row", None),
        P("row", None),
    )
    out_specs = (P(None, "row", None), P(None, "row", None), P("mode", None, "row", None))
    return jax.shard_map(
        on_device, mesh=mesh, in_specs=in_specs, out_specs=out_specs, check_vma=False
    )
```

```python
import functools
import math

import jax
import jax.numpy as jnp
import ml_dtypes
import numpy as np
from jax import lax
from jax.experimental import pallas as pl
from jax.experimental.pallas import tpu as pltpu
from jax.sharding import PartitionSpec as P

GRID = 1024
ROWS = 128
MESH = pl.DeviceIdType.MESH
F32 = jnp.float32
BF16 = jnp.bfloat16


@functools.cache
def propagator():
    u = np.arange(GRID)
    turns = u[:, None] * u[None, :] % GRID
    angles = np.minimum(turns, GRID - turns) * (2.0 * math.pi / GRID)
    sign = np.where(turns <= GRID // 2, 1.0, -1.0)
    cosine = np.cos(angles).astype(ml_dtypes.bfloat16).astype(np.float64)
    sine = (sign * np.sin(angles)).astype(ml_dtypes.bfloat16).astype(np.float64)
    f = (u + GRID // 2) % GRID - GRID // 2
    phases = (f * f % (2 * GRID)) * (math.pi / GRID)
    chirp = np.cos(phases) - 1j * np.sin(phases)
    h = ((cosine - 1j * sine) * chirp) @ (cosine + 1j * sine) / GRID
    return np.stack([h.real, h.imag]).astype(ml_dtypes.bfloat16)


def cos_sin(phase):
    x = phase * 0.5
    z = x * x
    s = [(-1.0) ** i / math.factorial(2 * i + 1) for i in range(7)]
    c = [(-1.0) ** i / math.factorial(2 * i) for i in range(7)]
    ps = jnp.full_like(z, s[-1])
    for v in s[-2::-1]:
        ps = ps * z + v
    pc = jnp.full_like(z, c[-1])
    for v in c[-2::-1]:
        pc = pc * z + v
    sn = ps * x
    return 1.0 - 2.0 * sn * sn, 2.0 * sn * pc


def fold(v):
    tiles = [
        v[r : r + 8, c : c + 128] for r in range(0, v.shape[0], 8) for c in range(0, v.shape[1], 128)
    ]
    while len(tiles) > 1:
        tiles = [sum(tiles[i : i + 2]) for i in range(0, len(tiles), 2)]
    return tiles[0]


def kernel(
    f_in, b1_in, b2_in, p1_in, p2_in, h_in, m1_out, m2_out, a_out,
    f, b, ph, w, wh, whrecv, h, hk, acc, raws, px, prod, raw, irecv, wrecv, part, zrecv, precv, prow,
    both, full, m1, m1recv, mask, g, yb, s, arr, ls, ss, rs,
):
    mode = lax.axis_index("mode")
    row = lax.axis_index("row")
    zl, yc = mode // 8, lax.rem(mode, 8)
    zh, x = row // 4, lax.rem(row, 4)

    def row_peer(k):
        return (mode, lax.rem(row + k, 8))

    def x_peer(k):
        return (mode, zh * 4 + lax.rem(x + k, 4))

    def yc_peer(k):
        return (zl * 8 + lax.rem(yc + k, 8), row)

    def z_peer(k):
        return (lax.rem(zl + k, 8) * 8 + yc, row)

    def z16_peer(k):
        z = lax.rem(zh * 8 + zl + k, 16)
        return (lax.rem(z, 8) * 8 + yc, (z // 8) * 4 + x)

    def y_peer(k):
        return (zl * 8 + lax.rem(yc + 2 * k, 8), row)

    def c_peer(k):
        return (mode + 1 - 2 * lax.rem(mode, 2), row)

    def xyc_peer(k):
        at = lax.rem(x * 8 + yc + k, 32)
        return (zl * 8 + lax.rem(at, 8), zh * 4 + at // 8)

    bar = pltpu.get_barrier_semaphore()

    def greet(last, peer):
        def body(k, _):
            pl.semaphore_signal(bar, inc=1, device_id=peer(k), device_id_type=MESH)
            return 0

        lax.fori_loop(1, last, body, 0)

    greet(8, row_peer)
    greet(16, z16_peer)
    greet(32, xyc_peer)

    loads = [
        pltpu.make_async_copy(src, dst, ls.at[i])
        for i, (src, dst) in enumerate(
            [(f_in, f), (b1_in, b.at[0]), (p1_in, ph.at[0]), (h_in, h), (b2_in, b.at[1]), (p2_in, ph.at[1])]
        )
    ]
    loads += [
        pltpu.make_async_copy(
            h_in.at[:, pl.ds(v * 256 + half * 128, 128), :],
            hk.at[:, half, pl.ds(v * 128, 128), :], ls.at[11 + half * 4 + v],
        )
        for half in range(2)
        for v in range(4)
    ]
    for c in loads:
        c.start()

    used = [0, 0]
    sent = []

    class Stage:
        def __init__(self, src, dst, peer, all_sent, all_came=None, came=1):
            self.src, self.dst, self.peer, self.all_came = src, dst, peer, all_came
            self.s, self.r = used
            used[0] += 1
            used[1] += came
            self.left = lambda: self.desc(0, 0, all_sent).wait_send()
            sent.append(self)

        def desc(self, k, slot=0, whole=None):
            return pltpu.make_async_remote_copy(
                src_ref=self.src(k) if whole is None else whole,
                dst_ref=self.dst(k) if whole is None else whole,
                send_sem=ss.at[self.s], recv_sem=rs.at[self.r + slot],
                device_id=self.peer(1), device_id_type=MESH,
            )

        def start(self, k, slot=0):
            pltpu.make_async_remote_copy(
                src_ref=self.src(k), dst_ref=self.dst(k), send_sem=ss.at[self.s],
                recv_sem=rs.at[self.r + slot], device_id=self.peer(k), device_id_type=MESH,
            ).start()

        def start_all(self, last, first=1):
            def body(k, _):
                self.start(k)
                return 0

            lax.fori_loop(first, last, body, 0)

        def wait(self, whole=None, slot=0):
            self.desc(0, slot, self.all_came if whole is None else whole).wait_recv()

    def sixteen(j):
        return pl.ds(pl.multiple_of(j * 16, 16), 16)

    def products(i, front, put, turned):
        back = b.at[i]

        def body(j, acc):
            rows = sixteen(j)
            fr, fi = front[0, rows, :].astype(F32), front[1, rows, :].astype(F32)
            br, bi = back[0, rows, :].astype(F32), back[1, rows, :].astype(F32)
            pr = br * fr + bi * fi
            pi = br * fi - bi * fr
            for q in range(8):
                cols = slice(q * 128, q * 128 + 128)
                put(j, q, jnp.stack([pr[:, cols], pi[:, cols]]).astype(BF16))
            if turned is None:
                return acc
            c, sn = turned(rows)
            return acc[0] + fold(pr * c - pi * sn), acc[1] + fold(pr * sn + pi * c)

        zero = jnp.zeros((8, 128), F32)
        ir, ii = lax.fori_loop(0, 8, body, (zero, zero))
        if turned is not None:
            irecv[i, 0, 0] = jnp.sum(ir, axis=0, keepdims=True)
            irecv[i, 0, 1] = jnp.sum(ii, axis=0, keepdims=True)

    def overlap(i):
        st = Stage(
            lambda k: irecv.at[i, 0], lambda k: irecv.at[i, k], row_peer,
            irecv.at[i, pl.ds(1, 7)], irecv.at[i, pl.ds(1, 7)],
        )
        st.start_all(8)
        return st

    def share_products(i):
        st = Stage(
            lambda k: prod.at[i, lax.rem(yc + k, 8)], lambda k: raw.at[i, k], yc_peer,
            raw.at[i, pl.ds(1, 7)], raw.at[i, pl.ds(1, 7)],
        )
        st.start_all(8)
        return st

    def share_weights(i):
        for q in range(2):
            wrecv[i, 0, q] = sum(irecv[i, k, q] for k in range(8))
        st = Stage(
            lambda k: wrecv.at[i, 0], lambda k: wrecv.at[i, k], yc_peer,
            wrecv.at[i, pl.ds(1, 7)], wrecv.at[i, pl.ds(1, 7)],
        )
        st.start_all(8)
        return st

    def reduced(i):
        weights = [
            [jnp.sum(wrecv[i, k, q], axis=1, keepdims=True) * (1.0 / GRID) for q in range(2)]
            for k in range(8)
        ]
        st = Stage(
            lambda k: part.at[i, k], lambda k: zrecv.at[i, k], z_peer,
            zrecv.at[i, pl.ds(1, 7)], zrecv.at[i, pl.ds(1, 7)],
        )

        def body(k, _):
            q = lax.rem(zl + k, 8)
            tr = jnp.zeros((16, 128), F32)
            ti = jnp.zeros((16, 128), F32)
            for m in range(8):
                pr, pi = raw[i, m, q, 0].astype(F32), raw[i, m, q, 1].astype(F32)
                wr, wi = weights[m]
                tr = tr + (wr * pr + wi * pi)
                ti = ti + (wr * pi - wi * pr)
            part[i, k, 0] = tr.astype(BF16)
            part[i, k, 1] = ti.astype(BF16)

            @pl.when(k < 8)
            def _():
                st.start(k)

            return 0

        lax.fori_loop(1, 9, body, 0)
        zrecv[i, 0] = part[i, 8]
        st.wait()
        return sum(zrecv[i, k].astype(F32) for k in range(8)).astype(BF16)

    def power_z(i, piece):
        v = piece.astype(F32)
        precv[i, 0] = jnp.sum(fold(v[0] * v[0] + v[1] * v[1]), axis=0, keepdims=True)
        st = Stage(
            lambda k: precv.at[i, 0], lambda k: precv.at[i, k], z16_peer,
            precv.at[i, pl.ds(1, 15)], precv.at[i, pl.ds(1, 15)],
        )
        st.start_all(16)
        return st

    def power_xy(i):
        prow[i, 0] = sum(precv[i, k] for k in range(16))
        st = Stage(
            lambda k: prow.at[i, 0], lambda k: prow.at[i, k], xyc_peer,
            prow.at[i, pl.ds(1, 31)], prow.at[i, pl.ds(1, 31)],
        )
        st.start_all(32)
        return st

    def power_floor(i):
        total = sum(prow[i, k] for k in range(32))
        mean = jnp.sum(total, axis=1, keepdims=True) * (1.0 / (GRID * GRID))
        return 0.25 * mean + 1e-6

    def masked(piece, floor):
        v = piece.astype(F32)
        scale = lax.rsqrt(v[0] * v[0] + v[1] * v[1] + floor)
        return (v[0] * scale).astype(BF16), (-v[1] * scale).astype(BF16)

    for c in loads[:3]:
        c.wait()

    def put_first(j, q, pair):
        px[q // 2, j // 4, lax.rem(j, 4) * 2 + q % 2] = pair

    products(0, f, put_first, lambda rows: cos_sin(ph[0, rows, :]))
    pl.semaphore_wait(bar, 7 + 15 + 31)
    over = overlap(0)
    turn = Stage(
        lambda k: px.at[lax.rem(x + k, 4)], lambda k: prod.at[0, pl.ds(2 * x, 2)], x_peer,
        prod.at[0, pl.ds(0, 6)], prod.at[0, pl.ds(0, 6)],
    )
    turn.start_all(4)

    def block(r, half):
        return pl.ds(pl.multiple_of(lax.rem(r, 4) * 256 + half * 128, 128), 128)

    moves = []
    parts = ((0, 0, 128), (1, 0, 64), (1, 64, 64))
    for half, top, size in parts:
        some = pl.ds(top, size)
        st = Stage(
            lambda k, half=half, some=some: f.at[:, some, block(row + k, half)],
            lambda k, half=half, some=some: raws.at[half, row, :, some, :], row_peer,
            raws.at[half, pl.ds(0, 7), :, some, :], raws.at[half, pl.ds(0, 7), :, some, :],
        )
        moves.append(st)

    def far(k):
        return (lax.rem(row + k, 8) // 4) != zh

    def move(part, want_far):
        def body(k, _):
            @pl.when(far(k) if want_far else jnp.logical_not(far(k)))
            def _():
                moves[part].start(k)

            return 0

        lax.fori_loop(1, 8, body, 0)

    move(0, True)
    own = [
        pltpu.make_async_copy(f.at[:, :, block(row, half)], raws.at[half, row], ls.at[9 + half])
        for half in range(2)
    ]
    for c in own:
        c.start()
    prod[0, pl.ds(2 * x, 2)] = px[x]
    turn.wait()
    share = share_products(0)
    for p in range(3):
        move(p, False)
    over.wait()
    weight = share_weights(0)
    raw[0, 0] = prod[0, yc]
    share.wait()
    weight.wait()
    piece = reduced(0)
    both[yc, 2 * zl + zh] = piece
    gather_z = Stage(
        lambda k: both.at[yc, 2 * zl + zh], lambda k: both.at[yc, 2 * zl + zh], z16_peer,
        both.at[yc, pl.ds(0, 15)], both.at[yc, pl.ds(0, 15)],
    )
    gather_z.start_all(16)
    pz = power_z(0, piece)
    gather_z.wait()
    move(1, True)
    move(2, True)
    gather_y = Stage(
        lambda k: both.at[yc], lambda k: both.at[yc], y_peer, both.at[pl.ds(0, 3)], None, 3
    )
    for o in range(1, 4):
        gather_y.start(o, o - 1)
    gather_c = Stage(
        lambda k: both.at[lax.rem(yc + 2 * k, 8)], lambda k: both.at[lax.rem(yc + 2 * k, 8)], c_peer,
        both.at[pl.ds(0, 4)], both.at[pl.ds(0, 4)],
    )
    gather_c.start(4)
    pz.wait()
    pxy = power_xy(0)
    for o in range(1, 4):
        gather_y.wait(both.at[0], o - 1)
        gather_c.start(4 - o)
    pxy.wait()
    floor = power_floor(0)
    gather_c.wait()

    def make_mask(n, _):
        for q in range(8):
            for z in range(2):
                mr, mi = masked(both[n, 2 * q + z], floor)
                both[n, 2 * q + z, 0] = mr
                both[n, 2 * q + z, 1] = mi
            m1[n, q] = both[n, 2 * q + zh]
        return 0

    early = [gather_z, gather_y, gather_c]
    for st in early:
        st.left()
    lax.fori_loop(0, 8, make_mask, 0)
    back1 = Stage(
        lambda k: m1.at[pl.ds(2 * lax.rem(x + k, 4), 2)], lambda k: m1recv.at[x], x_peer,
        m1recv.at[pl.ds(0, 3)], m1recv.at[pl.ds(0, 3)],
    )
    back1.start_all(4)
    m1recv[x] = m1[pl.ds(2 * x, 2)]
    for c in own:
        c.wait()
    for c in loads[3:]:
        c.wait()

    def turn_phase(j, _):
        rows = sixteen(j)
        c, sn = cos_sin(ph[1, rows, :])
        br, bi = b[1, 0, rows, :].astype(F32), b[1, 1, rows, :].astype(F32)
        w[0, rows, :] = (br * c + bi * sn).astype(BF16)
        w[1, rows, :] = (br * sn - bi * c).astype(BF16)
        return 0

    lax.fori_loop(0, 8, turn_phase, 0)
    turn_w = Stage(
        lambda k: wh.at[lax.rem(x + k, 4)], lambda k: whrecv.at[x], x_peer,
        whrecv.at[pl.ds(0, 3)], whrecv.at[pl.ds(0, 3)],
    )

    def adjoint(n, _):
        cols = pl.ds(pl.multiple_of(n * 256, 256), 256)
        field = w[...].reshape(2 * ROWS, GRID)
        a = jnp.dot(field, h[0, :, cols], preferred_element_type=F32)
        c = jnp.dot(field, h[1, :, cols], preferred_element_type=F32)
        wh[n, 0] = (a[:ROWS] - c[ROWS:]).astype(BF16)
        wh[n, 1] = (c[:ROWS] + a[ROWS:]).astype(BF16)
        return 0

    lax.fori_loop(0, 4, adjoint, 0)
    turn_w.start_all(4)
    whrecv[x] = wh[x]

    def columns(half, n, _):
        cols = pl.ds(pl.multiple_of(n * 256, 256), 256)
        field = s[half].reshape(2 * ROWS, GRID // 2)
        a = jnp.dot(field, hk[0, half, :, cols], preferred_element_type=F32)
        c = jnp.dot(field, hk[1, half, :, cols], preferred_element_type=F32)
        re, im = a[:ROWS] - c[ROWS:], c[:ROWS] + a[ROWS:]
        if half == 0:
            acc[0, :, cols] = re
            acc[1, :, cols] = im
        else:
            arr[0, :, cols] = (acc[0, :, cols] + re).astype(BF16)
            arr[1, :, cols] = (acc[1, :, cols] + im).astype(BF16)
        return 0

    for half in range(2):
        for p in (0,) if half == 0 else (1, 2):
            moves[p].wait()

        def apply(j, _, half=half):
            z, n = j // 8, lax.rem(j, 8)
            for u in range(4):
                v = both[n, (2 * u + half) * 2 + z].astype(F32)
                at = lax.rem(n, 2) * 64 + u * 16
                rows = pl.ds(pl.multiple_of(at, 16), 16)
                fr = raws[half, z * 4 + n // 2, 0, rows, :].astype(F32)
                fi = raws[half, z * 4 + n // 2, 1, rows, :].astype(F32)
                mr, mi = v[0], v[1]
                rows = pl.ds(pl.multiple_of(j * 64 + u * 16, 16), 16)
                g[half, rows, 0:128] = (fr * mr - fi * mi).astype(BF16)
                g[half, rows, 128:256] = (fr * mi + fi * mr).astype(BF16)
            return 0

        lax.fori_loop(0, 16, apply, 0)
        st = Stage(
            lambda k, half=half: yb.at[half, lax.rem(x + k, 4)],
            lambda k, half=half: s.at[half, :, :, pl.ds(pl.multiple_of(x * 128, 128), 128)],
            x_peer, yb.at[half, pl.ds(0, 3)], yb.at[half, pl.ds(0, 3)],
        )
        if half == 0:
            turn_w.wait()
            sums = [jnp.zeros((8, 128), F32) for _ in range(2)]
        for n in range(2):
            rows = pl.ds(pl.multiple_of(zh * 512 + n * 256, 256), 256)
            a = jnp.dot(h[0, rows, :], g[half], preferred_element_type=F32)
            c = jnp.dot(h[1, rows, :], g[half], preferred_element_type=F32)
            yr = (a[:, :128] - c[:, 128:]).astype(BF16)
            yi = (a[:, 128:] + c[:, :128]).astype(BF16)
            for e in range(2):
                to = 2 * n + e
                yb[half, to, 0] = yr[e * ROWS : e * ROWS + ROWS]
                yb[half, to, 1] = yi[e * ROWS : e * ROWS + ROWS]

                @pl.when(to != x)
                def _(to=to, st=st):
                    st.start(lax.rem(to - x + 4, 4))

            for e in range(2):
                to = 2 * n + e
                vr, vi = yb[half, to, 0].astype(F32), yb[half, to, 1].astype(F32)
                here = slice(half * 128, half * 128 + 128)
                ar, ai = whrecv[to, 0, :, here].astype(F32), whrecv[to, 1, :, here].astype(F32)
                sums[0] = sums[0] + fold(vr * ar - vi * ai)
                sums[1] = sums[1] + fold(vr * ai + vi * ar)

        s[half, :, :, pl.ds(pl.multiple_of(x * 128, 128), 128)] = yb[half, x]
        if half == 1:
            for q in range(2):
                irecv[1, 0, q] = jnp.sum(sums[q], axis=0, keepdims=True)
            over = overlap(1)
        st.wait()
        lax.fori_loop(0, 4, functools.partial(columns, half), 0)

    outs = [pltpu.make_async_copy(arr, a_out, ls.at[6])]
    outs[0].start()

    def put_second(j, q, pair):
        prod[1, j, q] = pair

    products(1, arr, put_second, None)
    share = share_products(1)
    over.wait()
    weight = share_weights(1)
    raw[1, 0] = prod[1, yc]
    share.wait()
    weight.wait()
    piece = reduced(1)
    full[yc, zl] = piece
    gather_z = Stage(
        lambda k: full.at[yc, zl], lambda k: full.at[yc, zl], z_peer, full.at[yc, pl.ds(0, 7)], None, 8
    )

    def spread(k, _):
        gather_z.start(k, zl)
        return 0

    pz = power_z(1, piece)
    lax.fori_loop(1, 8, spread, 0)

    gather_y2 = [
        Stage(lambda q: full.at[yc, q], lambda q: full.at[yc, q], lambda k, o=o: y_peer(o), full.at[yc], full.at[0])
        for o in range(1, 4)
    ]

    def onward(q):
        for st in gather_y2:
            st.start(q)

    onward(zl)

    def forward(d, _):
        for q in (zl - d, zl + d):

            @pl.when((q >= 0) & (q < 8))
            def _():
                gather_z.wait(full.at[yc, q], q)
                onward(q)

        return 0

    lax.fori_loop(1, 8, forward, 0)
    gather_c = Stage(
        lambda k: full.at[lax.rem(yc + 2 * k, 8)], lambda k: full.at[lax.rem(yc + 2 * k, 8)], c_peer,
        full.at[pl.ds(0, 4)], full.at[pl.ds(0, 4)],
    )
    gather_c.start(4)
    pz.wait()
    pxy = power_xy(1)
    for o in range(1, 4):
        gather_y2[o - 1].wait()
        gather_c.start(4 - o)

    back1.wait()

    def lay(j, _):
        for q in range(8):
            v = m1recv[q // 2, j // 4, lax.rem(j, 4) * 2 + q % 2]
            mask[0, 0, sixteen(j), q * 128 : q * 128 + 128] = v[0]
            mask[0, 1, sixteen(j), q * 128 : q * 128 + 128] = v[1]
        return 0

    lax.fori_loop(0, 8, lay, 0)
    outs.append(pltpu.make_async_copy(mask.at[0], m1_out, ls.at[7]))
    outs[1].start()
    pxy.wait()
    floor2 = power_floor(1)
    gather_c.wait()

    def finish(j, _):
        for q in range(8):
            mr, mi = masked(full[j, q], floor2)
            mask[1, 0, sixteen(j), q * 128 : q * 128 + 128] = mr
            mask[1, 1, sixteen(j), q * 128 : q * 128 + 128] = mi
        return 0

    lax.fori_loop(0, 8, finish, 0)
    outs.append(pltpu.make_async_copy(mask.at[1], m2_out, ls.at[8]))
    outs[2].start()
    for st in sent:
        if st not in early:
            st.left()
    for c in outs:
        c.wait()


def write_out(*refs):
    sems = refs[6]
    copies = []
    for src, dst in zip(refs[:3], refs[3:6]):
        for i in range(4):
            rows = pl.ds(i * 32, 32)
            copies.append(
                pltpu.make_async_copy(src.at[:, rows], dst.at[:, rows], sems.at[len(copies)])
            )
            copies[-1].start()
    for c in copies:
        c.wait()


def on_device(forward, backward_first, backward_second, phase_first, phase_second):
    hbm = pl.BlockSpec(memory_space=pl.ANY)
    block = (2, ROWS, GRID)
    tile = (2, 16, 128)
    m1, m2, arrived = pl.pallas_call(
        kernel,
        out_shape=[jax.ShapeDtypeStruct(block, BF16)] * 3,
        in_specs=[hbm] * 6,
        out_specs=[hbm] * 3,
        scratch_shapes=[
            pltpu.VMEM(block, BF16),
            pltpu.VMEM((2, *block), BF16),
            pltpu.VMEM((2, ROWS, GRID), F32),
            pltpu.VMEM(block, BF16),
            pltpu.VMEM((4, 2, ROWS, 256), BF16),
            pltpu.VMEM((4, 2, ROWS, 256), BF16),
            pltpu.VMEM((2, GRID, GRID), BF16),
            pltpu.VMEM((2, 2, GRID // 2, GRID), BF16),
            pltpu.VMEM(block, F32),
            pltpu.VMEM((2, 8, 2, ROWS, 128), BF16),
            pltpu.VMEM((4, 2, 8, *tile), BF16),
            pltpu.VMEM((2, 8, 8, *tile), BF16),
            pltpu.VMEM((2, 8, 8, *tile), BF16),
            pltpu.VMEM((2, 8, 2, 1, 128), F32),
            pltpu.VMEM((2, 8, 2, 1, 128), F32),
            pltpu.VMEM((2, 9, *tile), BF16),
            pltpu.VMEM((2, 8, *tile), BF16),
            pltpu.VMEM((2, 16, 1, 128), F32),
            pltpu.VMEM((2, 32, 1, 128), F32),
            pltpu.VMEM((8, 16, *tile), BF16),
            pltpu.VMEM((8, 8, *tile), BF16),
            pltpu.VMEM((8, 8, *tile), BF16),
            pltpu.VMEM((4, 2, 8, *tile), BF16),
            pltpu.VMEM((2, *block), BF16),
            pltpu.VMEM((2, GRID, 256), BF16),
            pltpu.VMEM((2, 4, 2, ROWS, 128), BF16),
            pltpu.VMEM((2, 2, ROWS, GRID // 2), BF16),
            pltpu.VMEM(block, BF16),
            pltpu.SemaphoreType.DMA((19,)),
            pltpu.SemaphoreType.DMA((32,)),
            pltpu.SemaphoreType.DMA((40,)),
        ],
        compiler_params=pltpu.CompilerParams(
            collective_id=0, has_side_effects=True, vmem_limit_bytes=52 * 2**20
        ),
    )(
        forward[0], backward_first[0], backward_second[0], phase_first, phase_second,
        jnp.asarray(propagator()),
    )
    m1, m2, arrived = pl.pallas_call(
        write_out,
        out_shape=[jax.ShapeDtypeStruct(block, BF16)] * 3,
        in_specs=[hbm] * 3,
        out_specs=[hbm] * 3,
        scratch_shapes=[pltpu.SemaphoreType.DMA((12,))],
        compiler_params=pltpu.CompilerParams(vmem_limit_bytes=2**20),
    )(m1, m2, arrived)
    return m1, m2, arrived[None]


def solution(mesh):
    in_specs = (
        P("mode", None, "row", None),
        P("mode", None, "row", None),
        P("mode", None, "row", None),
        P("row", None),
        P("row", None),
    )
    out_specs = (P(None, "row", None), P(None, "row", None), P("mode", None, "row", None))
    return jax.shard_map(
        on_device, mesh=mesh, in_specs=in_specs, out_specs=out_specs, check_vma=False
    )
```

```python
import functools
import math

import jax
import jax.numpy as jnp
import ml_dtypes
import numpy as np
from jax import lax
from jax.experimental import pallas as pl
from jax.experimental.pallas import tpu as pltpu
from jax.sharding import PartitionSpec as P

GRID = 1024
ROWS = 128
MESH = pl.DeviceIdType.MESH
F32 = jnp.float32
BF16 = jnp.bfloat16


@functools.cache
def propagator():
    u = np.arange(GRID)
    turns = u[:, None] * u[None, :] % GRID
    angles = np.minimum(turns, GRID - turns) * (2.0 * math.pi / GRID)
    sign = np.where(turns <= GRID // 2, 1.0, -1.0)
    cosine = np.cos(angles).astype(ml_dtypes.bfloat16).astype(np.float64)
    sine = (sign * np.sin(angles)).astype(ml_dtypes.bfloat16).astype(np.float64)
    f = (u + GRID // 2) % GRID - GRID // 2
    phases = (f * f % (2 * GRID)) * (math.pi / GRID)
    chirp = np.cos(phases) - 1j * np.sin(phases)
    h = ((cosine - 1j * sine) * chirp) @ (cosine + 1j * sine) / GRID
    return np.stack([h.real, h.imag]).astype(ml_dtypes.bfloat16)


def cos_sin(phase):
    x = phase * 0.5
    z = x * x
    s = [(-1.0) ** i / math.factorial(2 * i + 1) for i in range(7)]
    c = [(-1.0) ** i / math.factorial(2 * i) for i in range(7)]
    ps = jnp.full_like(z, s[-1])
    for v in s[-2::-1]:
        ps = ps * z + v
    pc = jnp.full_like(z, c[-1])
    for v in c[-2::-1]:
        pc = pc * z + v
    sn = ps * x
    return 1.0 - 2.0 * sn * sn, 2.0 * sn * pc


def fold(v):
    tiles = [
        v[r : r + 8, c : c + 128] for r in range(0, v.shape[0], 8) for c in range(0, v.shape[1], 128)
    ]
    while len(tiles) > 1:
        tiles = [sum(tiles[i : i + 2]) for i in range(0, len(tiles), 2)]
    return tiles[0]


def kernel(
    f_in, b1_in, b2_in, p1_in, p2_in, h_in, m1_out, m2_out, a_out,
    f, b, ph, w, wh, whrecv, h, hk, acc, raws, px, prod, raw, irecv, wrecv, part, zrecv, precv, prow,
    both, full, m1, m1recv, mask, g, yb, s, arr, ls, ss, rs,
):
    mode = lax.axis_index("mode")
    row = lax.axis_index("row")
    zl, yc = mode // 8, lax.rem(mode, 8)
    zh, x = row // 4, lax.rem(row, 4)

    def row_peer(k):
        return (mode, lax.rem(row + k, 8))

    def x_peer(k):
        return (mode, zh * 4 + lax.rem(x + k, 4))

    def yc_peer(k):
        return (zl * 8 + lax.rem(yc + k, 8), row)

    def z_peer(k):
        return (lax.rem(zl + k, 8) * 8 + yc, row)

    def z16_peer(k):
        z = lax.rem(zh * 8 + zl + k, 16)
        return (lax.rem(z, 8) * 8 + yc, (z // 8) * 4 + x)

    def y_peer(k):
        return (zl * 8 + lax.rem(yc + 2 * k, 8), row)

    def c_peer(k):
        return (mode + 1 - 2 * lax.rem(mode, 2), row)

    def xyc_peer(k):
        at = lax.rem(x * 8 + yc + k, 32)
        return (zl * 8 + lax.rem(at, 8), zh * 4 + at // 8)

    bar = pltpu.get_barrier_semaphore()

    def greet(last, peer):
        def body(k, _):
            pl.semaphore_signal(bar, inc=1, device_id=peer(k), device_id_type=MESH)
            return 0

        lax.fori_loop(1, last, body, 0)

    greet(8, row_peer)
    greet(16, z16_peer)
    greet(32, xyc_peer)

    loads = [
        pltpu.make_async_copy(src, dst, ls.at[i])
        for i, (src, dst) in enumerate(
            [(f_in, f), (b1_in, b.at[0]), (p1_in, ph.at[0]), (h_in, h), (b2_in, b.at[1]), (p2_in, ph.at[1])]
        )
    ]
    loads += [
        pltpu.make_async_copy(
            h_in.at[:, pl.ds(v * 256 + half * 128, 128), :],
            hk.at[:, half, pl.ds(v * 128, 128), :], ls.at[11 + half * 4 + v],
        )
        for half in range(2)
        for v in range(4)
    ]
    for c in loads:
        c.start()

    used = [0, 0]
    sent = []

    class Stage:
        def __init__(self, src, dst, peer, all_sent, all_came=None, came=1):
            self.src, self.dst, self.peer, self.all_came = src, dst, peer, all_came
            self.s, self.r = used
            used[0] += 1
            used[1] += came
            self.left = lambda: self.desc(0, 0, all_sent).wait_send()
            sent.append(self)

        def desc(self, k, slot=0, whole=None):
            return pltpu.make_async_remote_copy(
                src_ref=self.src(k) if whole is None else whole,
                dst_ref=self.dst(k) if whole is None else whole,
                send_sem=ss.at[self.s], recv_sem=rs.at[self.r + slot],
                device_id=self.peer(1), device_id_type=MESH,
            )

        def start(self, k, slot=0):
            pltpu.make_async_remote_copy(
                src_ref=self.src(k), dst_ref=self.dst(k), send_sem=ss.at[self.s],
                recv_sem=rs.at[self.r + slot], device_id=self.peer(k), device_id_type=MESH,
            ).start()

        def start_all(self, last, first=1):
            def body(k, _):
                self.start(k)
                return 0

            lax.fori_loop(first, last, body, 0)

        def wait(self, whole=None, slot=0):
            self.desc(0, slot, self.all_came if whole is None else whole).wait_recv()

    def sixteen(j):
        return pl.ds(pl.multiple_of(j * 16, 16), 16)

    def products(i, front, put, turned):
        back = b.at[i]

        def body(j, acc):
            rows = sixteen(j)
            fr, fi = front[0, rows, :].astype(F32), front[1, rows, :].astype(F32)
            br, bi = back[0, rows, :].astype(F32), back[1, rows, :].astype(F32)
            pr = br * fr + bi * fi
            pi = br * fi - bi * fr
            for q in range(8):
                cols = slice(q * 128, q * 128 + 128)
                put(j, q, jnp.stack([pr[:, cols], pi[:, cols]]).astype(BF16))
            if turned is None:
                return acc
            c, sn = turned(rows)
            return acc[0] + fold(pr * c - pi * sn), acc[1] + fold(pr * sn + pi * c)

        zero = jnp.zeros((8, 128), F32)
        ir, ii = lax.fori_loop(0, 8, body, (zero, zero))
        if turned is not None:
            irecv[i, 0, 0] = jnp.sum(ir, axis=0, keepdims=True)
            irecv[i, 0, 1] = jnp.sum(ii, axis=0, keepdims=True)

    def overlap(i):
        st = Stage(
            lambda k: irecv.at[i, 0], lambda k: irecv.at[i, k], row_peer,
            irecv.at[i, pl.ds(1, 7)], irecv.at[i, pl.ds(1, 7)],
        )
        st.start_all(8)
        return st

    def share_products(i):
        st = Stage(
            lambda k: prod.at[i, lax.rem(yc + k, 8)], lambda k: raw.at[i, k], yc_peer,
            raw.at[i, pl.ds(1, 7)], raw.at[i, pl.ds(1, 7)],
        )
        st.start_all(8)
        return st

    def share_weights(i):
        for q in range(2):
            wrecv[i, 0, q] = sum(irecv[i, k, q] for k in range(8))
        st = Stage(
            lambda k: wrecv.at[i, 0], lambda k: wrecv.at[i, k], yc_peer,
            wrecv.at[i, pl.ds(1, 7)], wrecv.at[i, pl.ds(1, 7)],
        )
        st.start_all(8)
        return st

    def reduced(i):
        weights = [
            [jnp.sum(wrecv[i, k, q], axis=1, keepdims=True) * (1.0 / GRID) for q in range(2)]
            for k in range(8)
        ]
        st = Stage(
            lambda k: part.at[i, k], lambda k: zrecv.at[i, k], z_peer,
            zrecv.at[i, pl.ds(1, 7)], zrecv.at[i, pl.ds(1, 7)],
        )

        def body(k, _):
            q = lax.rem(zl + k, 8)
            tr = jnp.zeros((16, 128), F32)
            ti = jnp.zeros((16, 128), F32)
            for m in range(8):
                pr, pi = raw[i, m, q, 0].astype(F32), raw[i, m, q, 1].astype(F32)
                wr, wi = weights[m]
                tr = tr + (wr * pr + wi * pi)
                ti = ti + (wr * pi - wi * pr)
            part[i, k, 0] = tr.astype(BF16)
            part[i, k, 1] = ti.astype(BF16)

            @pl.when(k < 8)
            def _():
                st.start(k)

            return 0

        lax.fori_loop(1, 9, body, 0)
        zrecv[i, 0] = part[i, 8]
        st.wait()
        return sum(zrecv[i, k].astype(F32) for k in range(8)).astype(BF16)

    def power_z(i, piece):
        v = piece.astype(F32)
        precv[i, 0] = jnp.sum(fold(v[0] * v[0] + v[1] * v[1]), axis=0, keepdims=True)
        st = Stage(
            lambda k: precv.at[i, 0], lambda k: precv.at[i, k], z16_peer,
            precv.at[i, pl.ds(1, 15)], precv.at[i, pl.ds(1, 15)],
        )
        st.start_all(16)
        return st

    def power_xy(i):
        prow[i, 0] = sum(precv[i, k] for k in range(16))
        st = Stage(
            lambda k: prow.at[i, 0], lambda k: prow.at[i, k], xyc_peer,
            prow.at[i, pl.ds(1, 31)], prow.at[i, pl.ds(1, 31)],
        )
        st.start_all(32)
        return st

    def power_floor(i):
        total = sum(prow[i, k] for k in range(32))
        mean = jnp.sum(total, axis=1, keepdims=True) * (1.0 / (GRID * GRID))
        return 0.25 * mean + 1e-6

    def masked(piece, floor):
        v = piece.astype(F32)
        scale = lax.rsqrt(v[0] * v[0] + v[1] * v[1] + floor)
        return (v[0] * scale).astype(BF16), (-v[1] * scale).astype(BF16)

    for c in loads[:3]:
        c.wait()

    def put_first(j, q, pair):
        px[q // 2, j // 4, lax.rem(j, 4) * 2 + q % 2] = pair

    products(0, f, put_first, lambda rows: cos_sin(ph[0, rows, :]))
    pl.semaphore_wait(bar, 7 + 15 + 31)
    over = overlap(0)
    turn = Stage(
        lambda k: px.at[lax.rem(x + k, 4)], lambda k: prod.at[0, pl.ds(2 * x, 2)], x_peer,
        prod.at[0, pl.ds(0, 6)], prod.at[0, pl.ds(0, 6)],
    )
    turn.start_all(4)

    def block(r, half):
        return pl.ds(pl.multiple_of(lax.rem(r, 4) * 256 + half * 128, 128), 128)

    moves = []
    parts = ((0, 0, 128), (1, 0, 64), (1, 64, 64))
    for half, top, size in parts:
        some = pl.ds(top, size)
        st = Stage(
            lambda k, half=half, some=some: f.at[:, some, block(row + k, half)],
            lambda k, half=half, some=some: raws.at[half, row, :, some, :], row_peer,
            raws.at[half, pl.ds(0, 7), :, some, :], raws.at[half, pl.ds(0, 7), :, some, :],
        )
        moves.append(st)

    def far(k):
        return (lax.rem(row + k, 8) // 4) != zh

    def move(part, want_far):
        def body(k, _):
            @pl.when(far(k) if want_far else jnp.logical_not(far(k)))
            def _():
                moves[part].start(k)

            return 0

        lax.fori_loop(1, 8, body, 0)

    move(0, True)
    own = [
        pltpu.make_async_copy(f.at[:, :, block(row, half)], raws.at[half, row], ls.at[9 + half])
        for half in range(2)
    ]
    for c in own:
        c.start()
    for c in loads[3:6]:
        c.wait()

    def turn_phase(j, _):
        rows = sixteen(j)
        c, sn = cos_sin(ph[1, rows, :])
        br, bi = b[1, 0, rows, :].astype(F32), b[1, 1, rows, :].astype(F32)
        w[0, rows, :] = (br * c + bi * sn).astype(BF16)
        w[1, rows, :] = (br * sn - bi * c).astype(BF16)
        return 0

    lax.fori_loop(0, 8, turn_phase, 0)
    turn_w = Stage(
        lambda k: wh.at[lax.rem(x + k, 4)], lambda k: whrecv.at[x], x_peer,
        whrecv.at[pl.ds(0, 3)], whrecv.at[pl.ds(0, 3)],
    )

    def adjoint(n, _):
        cols = pl.ds(pl.multiple_of(n * 256, 256), 256)
        field = w[...].reshape(2 * ROWS, GRID)
        a = jnp.dot(field, h[0, :, cols], preferred_element_type=F32)
        c = jnp.dot(field, h[1, :, cols], preferred_element_type=F32)
        wh[n, 0] = (a[:ROWS] - c[ROWS:]).astype(BF16)
        wh[n, 1] = (c[:ROWS] + a[ROWS:]).astype(BF16)
        return 0

    lax.fori_loop(0, 4, adjoint, 0)
    prod[0, pl.ds(2 * x, 2)] = px[x]
    turn.wait()
    share = share_products(0)
    for p in range(3):
        move(p, False)
    turn_w.start_all(4)
    whrecv[x] = wh[x]
    over.wait()
    weight = share_weights(0)
    raw[0, 0] = prod[0, yc]
    share.wait()
    weight.wait()
    piece = reduced(0)
    both[yc, 2 * zl + zh] = piece
    gather_z = Stage(
        lambda k: both.at[yc, 2 * zl + zh], lambda k: both.at[yc, 2 * zl + zh], z16_peer,
        both.at[yc, pl.ds(0, 15)], both.at[yc, pl.ds(0, 15)],
    )
    gather_z.start_all(16)
    pz = power_z(0, piece)
    gather_z.wait()
    move(1, True)
    move(2, True)
    gather_y = Stage(
        lambda k: both.at[yc], lambda k: both.at[yc], y_peer, both.at[pl.ds(0, 3)], None, 3
    )
    for o in range(1, 4):
        gather_y.start(o, o - 1)
    gather_c = Stage(
        lambda k: both.at[lax.rem(yc + 2 * k, 8)], lambda k: both.at[lax.rem(yc + 2 * k, 8)], c_peer,
        both.at[pl.ds(0, 4)], both.at[pl.ds(0, 4)],
    )
    gather_c.start(4)
    pz.wait()
    pxy = power_xy(0)
    for o in range(1, 4):
        gather_y.wait(both.at[0], o - 1)
        gather_c.start(4 - o)
    pxy.wait()
    floor = power_floor(0)
    gather_c.wait()

    def make_mask(n, _):
        for q in range(8):
            for z in range(2):
                mr, mi = masked(both[n, 2 * q + z], floor)
                both[n, 2 * q + z, 0] = mr
                both[n, 2 * q + z, 1] = mi
            m1[n, q] = both[n, 2 * q + zh]
        return 0

    early = [gather_z, gather_y, gather_c]
    for st in early:
        st.left()
    lax.fori_loop(0, 8, make_mask, 0)
    back1 = Stage(
        lambda k: m1.at[pl.ds(2 * lax.rem(x + k, 4), 2)], lambda k: m1recv.at[x], x_peer,
        m1recv.at[pl.ds(0, 3)], m1recv.at[pl.ds(0, 3)],
    )
    back1.start_all(4)
    m1recv[x] = m1[pl.ds(2 * x, 2)]
    for c in own:
        c.wait()
    for c in loads[6:]:
        c.wait()


    def columns(half, n, _):
        cols = pl.ds(pl.multiple_of(n * 256, 256), 256)
        field = s[half].reshape(2 * ROWS, GRID // 2)
        a = jnp.dot(field, hk[0, half, :, cols], preferred_element_type=F32)
        c = jnp.dot(field, hk[1, half, :, cols], preferred_element_type=F32)
        re, im = a[:ROWS] - c[ROWS:], c[:ROWS] + a[ROWS:]
        if half == 0:
            acc[0, :, cols] = re
            acc[1, :, cols] = im
        else:
            arr[0, :, cols] = (acc[0, :, cols] + re).astype(BF16)
            arr[1, :, cols] = (acc[1, :, cols] + im).astype(BF16)
        return 0

    for half in range(2):
        for p in (0,) if half == 0 else (1, 2):
            moves[p].wait()

        def apply(j, _, half=half):
            z, n = j // 8, lax.rem(j, 8)
            for u in range(4):
                v = both[n, (2 * u + half) * 2 + z].astype(F32)
                at = lax.rem(n, 2) * 64 + u * 16
                rows = pl.ds(pl.multiple_of(at, 16), 16)
                fr = raws[half, z * 4 + n // 2, 0, rows, :].astype(F32)
                fi = raws[half, z * 4 + n // 2, 1, rows, :].astype(F32)
                mr, mi = v[0], v[1]
                rows = pl.ds(pl.multiple_of(j * 64 + u * 16, 16), 16)
                g[half, rows, 0:128] = (fr * mr - fi * mi).astype(BF16)
                g[half, rows, 128:256] = (fr * mi + fi * mr).astype(BF16)
            return 0

        lax.fori_loop(0, 16, apply, 0)
        st = Stage(
            lambda k, half=half: yb.at[half, lax.rem(x + k, 4)],
            lambda k, half=half: s.at[half, :, :, pl.ds(pl.multiple_of(x * 128, 128), 128)],
            x_peer, yb.at[half, pl.ds(0, 3)], yb.at[half, pl.ds(0, 3)],
        )
        if half == 0:
            turn_w.wait()
            sums = [jnp.zeros((8, 128), F32) for _ in range(2)]
        for n in range(2):
            rows = pl.ds(pl.multiple_of(zh * 512 + n * 256, 256), 256)
            a = jnp.dot(h[0, rows, :], g[half], preferred_element_type=F32)
            c = jnp.dot(h[1, rows, :], g[half], preferred_element_type=F32)
            yr = (a[:, :128] - c[:, 128:]).astype(BF16)
            yi = (a[:, 128:] + c[:, :128]).astype(BF16)
            for e in range(2):
                to = 2 * n + e
                yb[half, to, 0] = yr[e * ROWS : e * ROWS + ROWS]
                yb[half, to, 1] = yi[e * ROWS : e * ROWS + ROWS]

                @pl.when(to != x)
                def _(to=to, st=st):
                    st.start(lax.rem(to - x + 4, 4))

            for e in range(2):
                to = 2 * n + e
                vr, vi = yb[half, to, 0].astype(F32), yb[half, to, 1].astype(F32)
                here = slice(half * 128, half * 128 + 128)
                ar, ai = whrecv[to, 0, :, here].astype(F32), whrecv[to, 1, :, here].astype(F32)
                sums[0] = sums[0] + fold(vr * ar - vi * ai)
                sums[1] = sums[1] + fold(vr * ai + vi * ar)

        s[half, :, :, pl.ds(pl.multiple_of(x * 128, 128), 128)] = yb[half, x]
        if half == 1:
            for q in range(2):
                irecv[1, 0, q] = jnp.sum(sums[q], axis=0, keepdims=True)
            over = overlap(1)
        st.wait()
        lax.fori_loop(0, 4, functools.partial(columns, half), 0)

    outs = [pltpu.make_async_copy(arr, a_out, ls.at[6])]
    outs[0].start()

    def put_second(j, q, pair):
        prod[1, j, q] = pair

    products(1, arr, put_second, None)
    share = share_products(1)
    over.wait()
    weight = share_weights(1)
    raw[1, 0] = prod[1, yc]
    share.wait()
    weight.wait()
    piece = reduced(1)
    full[yc, zl] = piece
    gather_z = Stage(
        lambda k: full.at[yc, zl], lambda k: full.at[yc, zl], z_peer, full.at[yc, pl.ds(0, 7)], None, 8
    )

    def spread(k, _):
        gather_z.start(k, zl)
        return 0

    pz = power_z(1, piece)
    lax.fori_loop(1, 8, spread, 0)

    gather_y2 = [
        Stage(lambda q: full.at[yc, q], lambda q: full.at[yc, q], lambda k, o=o: y_peer(o), full.at[yc], full.at[0])
        for o in range(1, 4)
    ]

    def onward(q):
        for st in gather_y2:
            st.start(q)

    onward(zl)

    def forward(d, _):
        for q in (zl - d, zl + d):

            @pl.when((q >= 0) & (q < 8))
            def _():
                gather_z.wait(full.at[yc, q], q)
                onward(q)

        return 0

    lax.fori_loop(1, 8, forward, 0)
    gather_c = Stage(
        lambda k: full.at[lax.rem(yc + 2 * k, 8)], lambda k: full.at[lax.rem(yc + 2 * k, 8)], c_peer,
        full.at[pl.ds(0, 4)], full.at[pl.ds(0, 4)],
    )
    gather_c.start(4)
    pz.wait()
    pxy = power_xy(1)
    for o in range(1, 4):
        gather_y2[o - 1].wait()
        gather_c.start(4 - o)

    back1.wait()

    def lay(j, _):
        for q in range(8):
            v = m1recv[q // 2, j // 4, lax.rem(j, 4) * 2 + q % 2]
            mask[0, 0, sixteen(j), q * 128 : q * 128 + 128] = v[0]
            mask[0, 1, sixteen(j), q * 128 : q * 128 + 128] = v[1]
        return 0

    lax.fori_loop(0, 8, lay, 0)
    outs.append(pltpu.make_async_copy(mask.at[0], m1_out, ls.at[7]))
    outs[1].start()
    pxy.wait()
    floor2 = power_floor(1)
    gather_c.wait()

    def finish(j, _):
        for q in range(8):
            mr, mi = masked(full[j, q], floor2)
            mask[1, 0, sixteen(j), q * 128 : q * 128 + 128] = mr
            mask[1, 1, sixteen(j), q * 128 : q * 128 + 128] = mi
        return 0

    lax.fori_loop(0, 8, finish, 0)
    outs.append(pltpu.make_async_copy(mask.at[1], m2_out, ls.at[8]))
    outs[2].start()
    for st in sent:
        if st not in early:
            st.left()
    for c in outs:
        c.wait()


def write_out(*refs):
    sems = refs[6]
    copies = []
    for src, dst in zip(refs[:3], refs[3:6]):
        for i in range(4):
            rows = pl.ds(i * 32, 32)
            copies.append(
                pltpu.make_async_copy(src.at[:, rows], dst.at[:, rows], sems.at[len(copies)])
            )
            copies[-1].start()
    for c in copies:
        c.wait()


def on_device(forward, backward_first, backward_second, phase_first, phase_second):
    hbm = pl.BlockSpec(memory_space=pl.ANY)
    block = (2, ROWS, GRID)
    tile = (2, 16, 128)
    m1, m2, arrived = pl.pallas_call(
        kernel,
        out_shape=[jax.ShapeDtypeStruct(block, BF16)] * 3,
        in_specs=[hbm] * 6,
        out_specs=[hbm] * 3,
        scratch_shapes=[
            pltpu.VMEM(block, BF16),
            pltpu.VMEM((2, *block), BF16),
            pltpu.VMEM((2, ROWS, GRID), F32),
            pltpu.VMEM(block, BF16),
            pltpu.VMEM((4, 2, ROWS, 256), BF16),
            pltpu.VMEM((4, 2, ROWS, 256), BF16),
            pltpu.VMEM((2, GRID, GRID), BF16),
            pltpu.VMEM((2, 2, GRID // 2, GRID), BF16),
            pltpu.VMEM(block, F32),
            pltpu.VMEM((2, 8, 2, ROWS, 128), BF16),
            pltpu.VMEM((4, 2, 8, *tile), BF16),
            pltpu.VMEM((2, 8, 8, *tile), BF16),
            pltpu.VMEM((2, 8, 8, *tile), BF16),
            pltpu.VMEM((2, 8, 2, 1, 128), F32),
            pltpu.VMEM((2, 8, 2, 1, 128), F32),
            pltpu.VMEM((2, 9, *tile), BF16),
            pltpu.VMEM((2, 8, *tile), BF16),
            pltpu.VMEM((2, 16, 1, 128), F32),
            pltpu.VMEM((2, 32, 1, 128), F32),
            pltpu.VMEM((8, 16, *tile), BF16),
            pltpu.VMEM((8, 8, *tile), BF16),
            pltpu.VMEM((8, 8, *tile), BF16),
            pltpu.VMEM((4, 2, 8, *tile), BF16),
            pltpu.VMEM((2, *block), BF16),
            pltpu.VMEM((2, GRID, 256), BF16),
            pltpu.VMEM((2, 4, 2, ROWS, 128), BF16),
            pltpu.VMEM((2, 2, ROWS, GRID // 2), BF16),
            pltpu.VMEM(block, BF16),
            pltpu.SemaphoreType.DMA((19,)),
            pltpu.SemaphoreType.DMA((32,)),
            pltpu.SemaphoreType.DMA((40,)),
        ],
        compiler_params=pltpu.CompilerParams(
            collective_id=0, has_side_effects=True, vmem_limit_bytes=52 * 2**20
        ),
    )(
        forward[0], backward_first[0], backward_second[0], phase_first, phase_second,
        jnp.asarray(propagator()),
    )
    m1, m2, arrived = pl.pallas_call(
        write_out,
        out_shape=[jax.ShapeDtypeStruct(block, BF16)] * 3,
        in_specs=[hbm] * 3,
        out_specs=[hbm] * 3,
        scratch_shapes=[pltpu.SemaphoreType.DMA((12,))],
        compiler_params=pltpu.CompilerParams(vmem_limit_bytes=2**20),
    )(m1, m2, arrived)
    return m1, m2, arrived[None]


def solution(mesh):
    in_specs = (
        P("mode", None, "row", None),
        P("mode", None, "row", None),
        P("mode", None, "row", None),
        P("row", None),
        P("row", None),
    )
    out_specs = (P(None, "row", None), P(None, "row", None), P("mode", None, "row", None))
    return jax.shard_map(
        on_device, mesh=mesh, in_specs=in_specs, out_specs=out_specs, check_vma=False
    )
```

```python
import functools
import math

import jax
import jax.numpy as jnp
import ml_dtypes
import numpy as np
from jax import lax
from jax.experimental import pallas as pl
from jax.experimental.pallas import tpu as pltpu
from jax.sharding import PartitionSpec as P

GRID = 1024
ROWS = 128
MESH = pl.DeviceIdType.MESH
F32 = jnp.float32
BF16 = jnp.bfloat16


@functools.cache
def propagator():
    u = np.arange(GRID)
    turns = u[:, None] * u[None, :] % GRID
    angles = np.minimum(turns, GRID - turns) * (2.0 * math.pi / GRID)
    sign = np.where(turns <= GRID // 2, 1.0, -1.0)
    cosine = np.cos(angles).astype(ml_dtypes.bfloat16).astype(np.float64)
    sine = (sign * np.sin(angles)).astype(ml_dtypes.bfloat16).astype(np.float64)
    f = (u + GRID // 2) % GRID - GRID // 2
    phases = (f * f % (2 * GRID)) * (math.pi / GRID)
    chirp = np.cos(phases) - 1j * np.sin(phases)
    h = ((cosine - 1j * sine) * chirp) @ (cosine + 1j * sine) / GRID
    return np.stack([h.real, h.imag]).astype(ml_dtypes.bfloat16)


def cos_sin(phase):
    x = phase * 0.5
    z = x * x
    s = [(-1.0) ** i / math.factorial(2 * i + 1) for i in range(7)]
    c = [(-1.0) ** i / math.factorial(2 * i) for i in range(7)]
    ps = jnp.full_like(z, s[-1])
    for v in s[-2::-1]:
        ps = ps * z + v
    pc = jnp.full_like(z, c[-1])
    for v in c[-2::-1]:
        pc = pc * z + v
    sn = ps * x
    return 1.0 - 2.0 * sn * sn, 2.0 * sn * pc


def fold(v):
    tiles = [
        v[r : r + 8, c : c + 128] for r in range(0, v.shape[0], 8) for c in range(0, v.shape[1], 128)
    ]
    while len(tiles) > 1:
        tiles = [sum(tiles[i : i + 2]) for i in range(0, len(tiles), 2)]
    return tiles[0]


def kernel(
    f_in, b1_in, b2_in, p1_in, p2_in, h_in, m1_out, m2_out, a_out,
    f, b, ph, w, wh, whrecv, h, hk, acc, raws, px, prod, raw, irecv, wrecv, part, zrecv, precv, prow,
    both, full, m1, m1recv, mask, g, yb, s, arr, ls, ss, rs,
):
    mode = lax.axis_index("mode")
    row = lax.axis_index("row")
    zl, yc = mode // 8, lax.rem(mode, 8)
    zh, x = row // 4, lax.rem(row, 4)

    def row_peer(k):
        return (mode, lax.rem(row + k, 8))

    def x_peer(k):
        return (mode, zh * 4 + lax.rem(x + k, 4))

    def yc_peer(k):
        return (zl * 8 + lax.rem(yc + k, 8), row)

    def z_peer(k):
        return (lax.rem(zl + k, 8) * 8 + yc, row)

    def z16_peer(k):
        z = lax.rem(zh * 8 + zl + k, 16)
        return (lax.rem(z, 8) * 8 + yc, (z // 8) * 4 + x)

    def y_peer(k):
        return (zl * 8 + lax.rem(yc + 2 * k, 8), row)

    def c_peer(k):
        return (mode + 1 - 2 * lax.rem(mode, 2), row)

    def xyc_peer(k):
        at = lax.rem(x * 8 + yc + k, 32)
        return (zl * 8 + lax.rem(at, 8), zh * 4 + at // 8)

    bar = pltpu.get_barrier_semaphore()

    def greet(last, peer):
        def body(k, _):
            pl.semaphore_signal(bar, inc=1, device_id=peer(k), device_id_type=MESH)
            return 0

        lax.fori_loop(1, last, body, 0)

    greet(8, row_peer)
    greet(16, z16_peer)
    greet(32, xyc_peer)

    loads = [
        pltpu.make_async_copy(src, dst, ls.at[i])
        for i, (src, dst) in enumerate(
            [(f_in, f), (b1_in, b.at[0]), (p1_in, ph.at[0]), (h_in, h), (b2_in, b.at[1]), (p2_in, ph.at[1])]
        )
    ]
    loads += [
        pltpu.make_async_copy(
            h_in.at[:, pl.ds(v * 256 + half * 128, 128), :],
            hk.at[:, half, pl.ds(v * 128, 128), :], ls.at[11 + half * 4 + v],
        )
        for half in range(2)
        for v in range(4)
    ]
    for c in loads:
        c.start()

    used = [0, 0]
    sent = []

    class Stage:
        def __init__(self, src, dst, peer, all_sent, all_came=None, came=1):
            self.src, self.dst, self.peer, self.all_came = src, dst, peer, all_came
            self.s, self.r = used
            used[0] += 1
            used[1] += came
            self.left = lambda: self.desc(0, 0, all_sent).wait_send()
            sent.append(self)

        def desc(self, k, slot=0, whole=None):
            return pltpu.make_async_remote_copy(
                src_ref=self.src(k) if whole is None else whole,
                dst_ref=self.dst(k) if whole is None else whole,
                send_sem=ss.at[self.s], recv_sem=rs.at[self.r + slot],
                device_id=self.peer(1), device_id_type=MESH,
            )

        def start(self, k, slot=0):
            pltpu.make_async_remote_copy(
                src_ref=self.src(k), dst_ref=self.dst(k), send_sem=ss.at[self.s],
                recv_sem=rs.at[self.r + slot], device_id=self.peer(k), device_id_type=MESH,
            ).start()

        def start_all(self, last, first=1):
            def body(k, _):
                self.start(k)
                return 0

            lax.fori_loop(first, last, body, 0)

        def wait(self, whole=None, slot=0):
            self.desc(0, slot, self.all_came if whole is None else whole).wait_recv()

    def sixteen(j):
        return pl.ds(pl.multiple_of(j * 16, 16), 16)

    def products(i, front, put, turned):
        back = b.at[i]

        def body(j, acc):
            rows = sixteen(j)
            fr, fi = front[0, rows, :].astype(F32), front[1, rows, :].astype(F32)
            br, bi = back[0, rows, :].astype(F32), back[1, rows, :].astype(F32)
            pr = br * fr + bi * fi
            pi = br * fi - bi * fr
            for q in range(8):
                cols = slice(q * 128, q * 128 + 128)
                put(j, q, jnp.stack([pr[:, cols], pi[:, cols]]).astype(BF16))
            if turned is None:
                return acc
            c, sn = turned(rows)
            return acc[0] + fold(pr * c - pi * sn), acc[1] + fold(pr * sn + pi * c)

        zero = jnp.zeros((8, 128), F32)
        ir, ii = lax.fori_loop(0, 8, body, (zero, zero))
        if turned is not None:
            irecv[i, 0, 0] = jnp.sum(ir, axis=0, keepdims=True)
            irecv[i, 0, 1] = jnp.sum(ii, axis=0, keepdims=True)

    def overlap(i):
        st = Stage(
            lambda k: irecv.at[i, 0], lambda k: irecv.at[i, k], row_peer,
            irecv.at[i, pl.ds(1, 7)], irecv.at[i, pl.ds(1, 7)],
        )
        st.start_all(8)
        return st

    def share_products(i):
        st = Stage(
            lambda k: prod.at[i, lax.rem(yc + k, 8)], lambda k: raw.at[i, k], yc_peer,
            raw.at[i, pl.ds(1, 7)], raw.at[i, pl.ds(1, 7)],
        )
        st.start_all(8)
        return st

    def share_weights(i):
        for q in range(2):
            wrecv[i, 0, q] = sum(irecv[i, k, q] for k in range(8))
        st = Stage(
            lambda k: wrecv.at[i, 0], lambda k: wrecv.at[i, k], yc_peer,
            wrecv.at[i, pl.ds(1, 7)], wrecv.at[i, pl.ds(1, 7)],
        )
        st.start_all(8)
        return st

    def reduced(i):
        weights = [
            [jnp.sum(wrecv[i, k, q], axis=1, keepdims=True) * (1.0 / GRID) for q in range(2)]
            for k in range(8)
        ]
        st = Stage(
            lambda k: part.at[i, k], lambda k: zrecv.at[i, k], z_peer,
            zrecv.at[i, pl.ds(1, 7)], zrecv.at[i, pl.ds(1, 7)],
        )

        def body(k, _):
            q = lax.rem(zl + k, 8)
            tr = jnp.zeros((16, 128), F32)
            ti = jnp.zeros((16, 128), F32)
            for m in range(8):
                pr, pi = raw[i, m, q, 0].astype(F32), raw[i, m, q, 1].astype(F32)
                wr, wi = weights[m]
                tr = tr + (wr * pr + wi * pi)
                ti = ti + (wr * pi - wi * pr)
            part[i, k, 0] = tr.astype(BF16)
            part[i, k, 1] = ti.astype(BF16)

            @pl.when(k < 8)
            def _():
                st.start(k)

            return 0

        lax.fori_loop(1, 9, body, 0)
        zrecv[i, 0] = part[i, 8]
        st.wait()
        return sum(zrecv[i, k].astype(F32) for k in range(8)).astype(BF16)

    def power_z(i, piece):
        v = piece.astype(F32)
        precv[i, 0] = jnp.sum(fold(v[0] * v[0] + v[1] * v[1]), axis=0, keepdims=True)
        st = Stage(
            lambda k: precv.at[i, 0], lambda k: precv.at[i, k], z16_peer,
            precv.at[i, pl.ds(1, 15)], precv.at[i, pl.ds(1, 15)],
        )
        st.start_all(16)
        return st

    def power_xy(i):
        prow[i, 0] = sum(precv[i, k] for k in range(16))
        st = Stage(
            lambda k: prow.at[i, 0], lambda k: prow.at[i, k], xyc_peer,
            prow.at[i, pl.ds(1, 31)], prow.at[i, pl.ds(1, 31)],
        )
        st.start_all(32)
        return st

    def power_floor(i):
        total = sum(prow[i, k] for k in range(32))
        mean = jnp.sum(total, axis=1, keepdims=True) * (1.0 / (GRID * GRID))
        return 0.25 * mean + 1e-6

    def masked(piece, floor):
        v = piece.astype(F32)
        scale = lax.rsqrt(v[0] * v[0] + v[1] * v[1] + floor)
        return (v[0] * scale).astype(BF16), (-v[1] * scale).astype(BF16)

    for c in loads[:3]:
        c.wait()

    def put_first(j, q, pair):
        px[q // 2, j // 4, lax.rem(j, 4) * 2 + q % 2] = pair

    products(0, f, put_first, lambda rows: cos_sin(ph[0, rows, :]))
    pl.semaphore_wait(bar, 7 + 15 + 31)
    over = overlap(0)
    turn = Stage(
        lambda k: px.at[lax.rem(x + k, 4)], lambda k: prod.at[0, pl.ds(2 * x, 2)], x_peer,
        prod.at[0, pl.ds(0, 6)], prod.at[0, pl.ds(0, 6)],
    )
    turn.start_all(4)

    def block(r, half):
        return pl.ds(pl.multiple_of(lax.rem(r, 4) * 256 + half * 128, 128), 128)

    moves = []
    parts = ((0, 0, 128), (1, 0, 64), (1, 64, 64))
    for half, top, size in parts:
        some = pl.ds(top, size)
        st = Stage(
            lambda k, half=half, some=some: f.at[:, some, block(row + k, half)],
            lambda k, half=half, some=some: raws.at[half, row, :, some, :], row_peer,
            raws.at[half, pl.ds(0, 7), :, some, :], raws.at[half, pl.ds(0, 7), :, some, :],
        )
        moves.append(st)

    def far(k):
        return (lax.rem(row + k, 8) // 4) != zh

    def move(part, want_far):
        def body(k, _):
            @pl.when(far(k) if want_far else jnp.logical_not(far(k)))
            def _():
                moves[part].start(k)

            return 0

        lax.fori_loop(1, 8, body, 0)

    move(0, True)
    own = [
        pltpu.make_async_copy(f.at[:, :, block(row, half)], raws.at[half, row], ls.at[9 + half])
        for half in range(2)
    ]
    for c in own:
        c.start()
    for c in loads[3:6]:
        c.wait()

    def turn_phase(j, _):
        rows = sixteen(j)
        c, sn = cos_sin(ph[1, rows, :])
        br, bi = b[1, 0, rows, :].astype(F32), b[1, 1, rows, :].astype(F32)
        w[0, rows, :] = (br * c + bi * sn).astype(BF16)
        w[1, rows, :] = (br * sn - bi * c).astype(BF16)
        return 0

    lax.fori_loop(0, 8, turn_phase, 0)
    turn_w = Stage(
        lambda k: wh.at[lax.rem(x + k, 4)], lambda k: whrecv.at[x], x_peer,
        whrecv.at[pl.ds(0, 3)], whrecv.at[pl.ds(0, 3)],
    )

    def adjoint(n, _):
        cols = pl.ds(pl.multiple_of(n * 256, 256), 256)
        field = w[...].reshape(2 * ROWS, GRID)
        a = jnp.dot(field, h[0, :, cols], preferred_element_type=F32)
        c = jnp.dot(field, h[1, :, cols], preferred_element_type=F32)
        wh[n, 0] = (a[:ROWS] - c[ROWS:]).astype(BF16)
        wh[n, 1] = (c[:ROWS] + a[ROWS:]).astype(BF16)
        return 0

    lax.fori_loop(0, 4, adjoint, 0)
    prod[0, pl.ds(2 * x, 2)] = px[x]
    turn.wait()
    share = share_products(0)
    for p in range(3):
        move(p, False)
    turn_w.start_all(4)
    whrecv[x] = wh[x]
    over.wait()
    weight = share_weights(0)
    raw[0, 0] = prod[0, yc]
    share.wait()
    weight.wait()
    piece = reduced(0)
    both[yc, 2 * zl + zh] = piece
    gather_z = Stage(
        lambda k: both.at[yc, 2 * zl + zh], lambda k: both.at[yc, 2 * zl + zh], z16_peer,
        both.at[yc, pl.ds(0, 15)], both.at[yc, pl.ds(0, 15)],
    )
    gather_z.start_all(16)
    pz = power_z(0, piece)
    gather_z.wait()
    move(1, True)
    move(2, True)
    gather_y = Stage(
        lambda k: both.at[yc], lambda k: both.at[yc], y_peer, both.at[pl.ds(0, 3)], None, 3
    )
    for o in range(1, 4):
        gather_y.start(o, o - 1)
    gather_c = Stage(
        lambda k: both.at[lax.rem(yc + 2 * k, 8)], lambda k: both.at[lax.rem(yc + 2 * k, 8)], c_peer,
        both.at[pl.ds(0, 4)], both.at[pl.ds(0, 4)],
    )
    gather_c.start(4)
    pz.wait()
    pxy = power_xy(0)
    for o in range(1, 4):
        gather_y.wait(both.at[0], o - 1)
        gather_c.start(4 - o)
    pxy.wait()
    floor = power_floor(0)
    gather_c.wait()

    def make_mask(n, _):
        for q in range(8):
            for z in range(2):
                mr, mi = masked(both[n, 2 * q + z], floor)
                both[n, 2 * q + z, 0] = mr
                both[n, 2 * q + z, 1] = mi
            m1[n, q] = both[n, 2 * q + zh]
        return 0

    early = [gather_z, gather_y, gather_c]
    for st in early:
        st.left()
    lax.fori_loop(0, 8, make_mask, 0)
    back1 = Stage(
        lambda k: m1.at[pl.ds(2 * lax.rem(x + k, 4), 2)], lambda k: m1recv.at[x], x_peer,
        m1recv.at[pl.ds(0, 3)], m1recv.at[pl.ds(0, 3)],
    )
    back1.start_all(4)
    m1recv[x] = m1[pl.ds(2 * x, 2)]
    for c in own:
        c.wait()
    for c in loads[6:]:
        c.wait()


    to_rows = []

    def columns(half, n, _):
        cols = pl.ds(pl.multiple_of(n * 256, 256), 256)
        field = s[half].reshape(2 * ROWS, GRID // 2)
        a = jnp.dot(field, hk[0, half, :, cols], preferred_element_type=F32)
        c = jnp.dot(field, hk[1, half, :, cols], preferred_element_type=F32)
        re, im = a[:ROWS] - c[ROWS:], c[:ROWS] + a[ROWS:]
        if half == 0:
            acc[0, :, cols] = re
            acc[1, :, cols] = im
        else:
            arr[0, :, cols] = (acc[0, :, cols] + re).astype(BF16)
            arr[1, :, cols] = (acc[1, :, cols] + im).astype(BF16)
        return 0

    for half in range(2):
        for p in (0,) if half == 0 else (1, 2):
            moves[p].wait()

        def apply(j, _, half=half):
            z, n = j // 8, lax.rem(j, 8)
            for u in range(4):
                v = both[n, (2 * u + half) * 2 + z].astype(F32)
                at = lax.rem(n, 2) * 64 + u * 16
                rows = pl.ds(pl.multiple_of(at, 16), 16)
                fr = raws[half, z * 4 + n // 2, 0, rows, :].astype(F32)
                fi = raws[half, z * 4 + n // 2, 1, rows, :].astype(F32)
                mr, mi = v[0], v[1]
                rows = pl.ds(pl.multiple_of(j * 64 + u * 16, 16), 16)
                g[half, rows, 0:128] = (fr * mr - fi * mi).astype(BF16)
                g[half, rows, 128:256] = (fr * mi + fi * mr).astype(BF16)
            return 0

        lax.fori_loop(0, 16, apply, 0)
        st = Stage(
            lambda k, half=half: yb.at[half, lax.rem(x + k, 4)],
            lambda k, half=half: s.at[half, :, :, pl.ds(pl.multiple_of(x * 128, 128), 128)],
            x_peer, yb.at[half, pl.ds(0, 3)], yb.at[half, pl.ds(0, 3)],
        )
        if half == 0:
            turn_w.wait()
            sums = [jnp.zeros((8, 128), F32) for _ in range(2)]
        for n in range(2):
            rows = pl.ds(pl.multiple_of(zh * 512 + n * 256, 256), 256)
            a = jnp.dot(h[0, rows, :], g[half], preferred_element_type=F32)
            c = jnp.dot(h[1, rows, :], g[half], preferred_element_type=F32)
            yr = (a[:, :128] - c[:, 128:]).astype(BF16)
            yi = (a[:, 128:] + c[:, :128]).astype(BF16)
            for e in range(2):
                to = 2 * n + e
                yb[half, to, 0] = yr[e * ROWS : e * ROWS + ROWS]
                yb[half, to, 1] = yi[e * ROWS : e * ROWS + ROWS]

                @pl.when(to != x)
                def _(to=to, st=st):
                    st.start(lax.rem(to - x + 4, 4))

            for e in range(2):
                to = 2 * n + e
                vr, vi = yb[half, to, 0].astype(F32), yb[half, to, 1].astype(F32)
                here = slice(half * 128, half * 128 + 128)
                ar, ai = whrecv[to, 0, :, here].astype(F32), whrecv[to, 1, :, here].astype(F32)
                sums[0] = sums[0] + fold(vr * ar - vi * ai)
                sums[1] = sums[1] + fold(vr * ai + vi * ar)

        s[half, :, :, pl.ds(pl.multiple_of(x * 128, 128), 128)] = yb[half, x]
        if half == 1:
            for q in range(2):
                irecv[1, 0, q] = jnp.sum(sums[q], axis=0, keepdims=True)
            over = overlap(1)
        to_rows.append(st)

    for half in range(2):
        to_rows[half].wait()
        lax.fori_loop(0, 4, functools.partial(columns, half), 0)

    outs = [pltpu.make_async_copy(arr, a_out, ls.at[6])]
    outs[0].start()

    def put_second(j, q, pair):
        prod[1, j, q] = pair

    products(1, arr, put_second, None)
    share = share_products(1)
    over.wait()
    weight = share_weights(1)
    raw[1, 0] = prod[1, yc]
    share.wait()
    weight.wait()
    piece = reduced(1)
    full[yc, zl] = piece
    gather_z = Stage(
        lambda k: full.at[yc, zl], lambda k: full.at[yc, zl], z_peer, full.at[yc, pl.ds(0, 7)], None, 8
    )

    def spread(k, _):
        gather_z.start(k, zl)
        return 0

    pz = power_z(1, piece)
    lax.fori_loop(1, 8, spread, 0)

    gather_y2 = [
        Stage(lambda q: full.at[yc, q], lambda q: full.at[yc, q], lambda k, o=o: y_peer(o), full.at[yc], full.at[0])
        for o in range(1, 4)
    ]

    def onward(q):
        for st in gather_y2:
            st.start(q)

    onward(zl)

    def forward(d, _):
        for q in (zl - d, zl + d):

            @pl.when((q >= 0) & (q < 8))
            def _():
                gather_z.wait(full.at[yc, q], q)
                onward(q)

        return 0

    lax.fori_loop(1, 8, forward, 0)
    gather_c = Stage(
        lambda k: full.at[lax.rem(yc + 2 * k, 8)], lambda k: full.at[lax.rem(yc + 2 * k, 8)], c_peer,
        full.at[pl.ds(0, 4)], full.at[pl.ds(0, 4)],
    )
    gather_c.start(4)
    pz.wait()
    pxy = power_xy(1)
    for o in range(1, 4):
        gather_y2[o - 1].wait()
        gather_c.start(4 - o)

    back1.wait()

    def lay(j, _):
        for q in range(8):
            v = m1recv[q // 2, j // 4, lax.rem(j, 4) * 2 + q % 2]
            mask[0, 0, sixteen(j), q * 128 : q * 128 + 128] = v[0]
            mask[0, 1, sixteen(j), q * 128 : q * 128 + 128] = v[1]
        return 0

    lax.fori_loop(0, 8, lay, 0)
    outs.append(pltpu.make_async_copy(mask.at[0], m1_out, ls.at[7]))
    outs[1].start()
    pxy.wait()
    floor2 = power_floor(1)
    gather_c.wait()

    def finish(j, _):
        for q in range(8):
            mr, mi = masked(full[j, q], floor2)
            mask[1, 0, sixteen(j), q * 128 : q * 128 + 128] = mr
            mask[1, 1, sixteen(j), q * 128 : q * 128 + 128] = mi
        return 0

    lax.fori_loop(0, 8, finish, 0)
    outs.append(pltpu.make_async_copy(mask.at[1], m2_out, ls.at[8]))
    outs[2].start()
    for st in sent:
        if st not in early:
            st.left()
    for c in outs:
        c.wait()


def write_out(*refs):
    sems = refs[6]
    copies = []
    for src, dst in zip(refs[:3], refs[3:6]):
        for i in range(4):
            rows = pl.ds(i * 32, 32)
            copies.append(
                pltpu.make_async_copy(src.at[:, rows], dst.at[:, rows], sems.at[len(copies)])
            )
            copies[-1].start()
    for c in copies:
        c.wait()


def on_device(forward, backward_first, backward_second, phase_first, phase_second):
    hbm = pl.BlockSpec(memory_space=pl.ANY)
    block = (2, ROWS, GRID)
    tile = (2, 16, 128)
    m1, m2, arrived = pl.pallas_call(
        kernel,
        out_shape=[jax.ShapeDtypeStruct(block, BF16)] * 3,
        in_specs=[hbm] * 6,
        out_specs=[hbm] * 3,
        scratch_shapes=[
            pltpu.VMEM(block, BF16),
            pltpu.VMEM((2, *block), BF16),
            pltpu.VMEM((2, ROWS, GRID), F32),
            pltpu.VMEM(block, BF16),
            pltpu.VMEM((4, 2, ROWS, 256), BF16),
            pltpu.VMEM((4, 2, ROWS, 256), BF16),
            pltpu.VMEM((2, GRID, GRID), BF16),
            pltpu.VMEM((2, 2, GRID // 2, GRID), BF16),
            pltpu.VMEM(block, F32),
            pltpu.VMEM((2, 8, 2, ROWS, 128), BF16),
            pltpu.VMEM((4, 2, 8, *tile), BF16),
            pltpu.VMEM((2, 8, 8, *tile), BF16),
            pltpu.VMEM((2, 8, 8, *tile), BF16),
            pltpu.VMEM((2, 8, 2, 1, 128), F32),
            pltpu.VMEM((2, 8, 2, 1, 128), F32),
            pltpu.VMEM((2, 9, *tile), BF16),
            pltpu.VMEM((2, 8, *tile), BF16),
            pltpu.VMEM((2, 16, 1, 128), F32),
            pltpu.VMEM((2, 32, 1, 128), F32),
            pltpu.VMEM((8, 16, *tile), BF16),
            pltpu.VMEM((8, 8, *tile), BF16),
            pltpu.VMEM((8, 8, *tile), BF16),
            pltpu.VMEM((4, 2, 8, *tile), BF16),
            pltpu.VMEM((2, *block), BF16),
            pltpu.VMEM((2, GRID, 256), BF16),
            pltpu.VMEM((2, 4, 2, ROWS, 128), BF16),
            pltpu.VMEM((2, 2, ROWS, GRID // 2), BF16),
            pltpu.VMEM(block, BF16),
            pltpu.SemaphoreType.DMA((19,)),
            pltpu.SemaphoreType.DMA((32,)),
            pltpu.SemaphoreType.DMA((40,)),
        ],
        compiler_params=pltpu.CompilerParams(
            collective_id=0, has_side_effects=True, vmem_limit_bytes=52 * 2**20
        ),
    )(
        forward[0], backward_first[0], backward_second[0], phase_first, phase_second,
        jnp.asarray(propagator()),
    )
    m1, m2, arrived = pl.pallas_call(
        write_out,
        out_shape=[jax.ShapeDtypeStruct(block, BF16)] * 3,
        in_specs=[hbm] * 3,
        out_specs=[hbm] * 3,
        scratch_shapes=[pltpu.SemaphoreType.DMA((12,))],
        compiler_params=pltpu.CompilerParams(vmem_limit_bytes=2**20),
    )(m1, m2, arrived)
    return m1, m2, arrived[None]


def solution(mesh):
    in_specs = (
        P("mode", None, "row", None),
        P("mode", None, "row", None),
        P("mode", None, "row", None),
        P("row", None),
        P("row", None),
    )
    out_specs = (P(None, "row", None), P(None, "row", None), P("mode", None, "row", None))
    return jax.shard_map(
        on_device, mesh=mesh, in_specs=in_specs, out_specs=out_specs, check_vma=False
    )
```
